1024 devices in a mesh: tower: 16 (over y, core), hst: 64 (over x, z).
Axes of the slice: x: 4, y: 8, z: 16, core: 2. Of those that a mesh axis runs over, the one named last changes fastest.
Arguments:
- top_grad: bfloat16 [2048, 64, 256], P(('tower', 'hst')), may hold values from -6 to 6
- pooled_in: bfloat16 [64, 2048, 2048], P('hst', 'tower'), may hold values from -6 to 6
- w_down: bfloat16 [64, 2048, 256], P('hst'), may hold values from -0.125 to 0.125
- w_up: bfloat16 [64, 256, 2048], P('hst'), may hold values from -0.375 to 0.375
- cross_bias: float32 [64, 2048], P('hst'), may hold values from -3 to 3
- w_comp: bfloat16 [64, 2048, 256], P('hst'), may hold values from -0.375 to 0.375
- feature_slot: int32 [64, 16], P('hst'), may hold values from 0 to 15, each once within a row
- bag_ids: int32 [64, 16, 2048, 8], P('hst', 'tower'), may hold values from 0 to 511
- bag_lengths: int32 [64, 16, 2048], P('hst', 'tower'), may hold values from 1 to 8
Outputs:
- grad_down: float32 [64, 2048, 256], P('hst', 'tower')
- grad_up: float32 [64, 256, 2048], P('hst', None, 'tower')
- grad_bias: float32 [64, 2048], P('hst', 'tower')
- grad_comp: float32 [64, 2048, 256], P('hst', 'tower')
- table_grads: float32 [64, 16, 512, 128], P('hst', 'tower')
The draws below stay inside these ranges and needn't reach their ends.
Inputs may be any that keep to these rules, and one draw needn't show every extreme that they name: `feature_slot`: each of a tower module's slots holds another table. `bag_ids`: slots at or past a bag's length hold row ids that count for nothing.
All inputs are finite; a program needn't handle non-finite values.
Results may differ from the reference program's by a relative error of at most 0.0065.
Values may be sent and summed in bfloat16 or wider, within the bound.
No kernel may reach another device: no remote copies, remote signals or barrier semaphores. Data moves between devices by JAX's collectives and lax.ppermute only.
A program may use at most 32 MiB of HBM per device.

```python
import math
import jax
import jax.numpy as jnp
import numpy as np
from jax import lax

EMBED = 128
FEATS = 16
COMP = 256
RANK = 256
TABLE_ROWS = 512
SLOTS = 8
WIDTH = 2048
GROUPS = 64
BATCH = 2048


def place_ends(result, key, low, largest):
    extent = result.shape
    index_at = [jax.random.randint(jax.random.fold_in(key, axis), (), 0, extent[axis]) for axis in range(len(extent))]
    result = result.at[tuple(index_at)].set(low)
    longest = extent.index(max(extent))
    index_at[longest] = (index_at[longest] + 1) % extent[longest]
    return result.at[tuple(index_at)].set(largest)


def raised(drawn, own_key, source, target, shards_of, factor):
    def block_of(axis_at):
        return (jnp.arange(drawn.shape[axis_at]) // (drawn.shape[axis_at] // shards_of)).reshape((-1,) + (1,) * (drawn.ndim - 1 - axis_at))

    one_side = jax.random.permutation(own_key, shards_of)[block_of(target)]
    second = (block_of(target) + shards_of // 2) % shards_of
    return jnp.where((block_of(source) == one_side) | (block_of(source) == second), factor * drawn, drawn)


def level_of(own_key, dims, pieces, least, largest):
    gain = 1.0
    for axis_at, parts in pieces:
        draws = jax.random.uniform(jax.random.fold_in(jax.random.fold_in(own_key, 6), axis_at), (parts,), jnp.float32, least / len(pieces), largest / len(pieces))
        gain = gain * jnp.repeat(jnp.exp(draws), dims[axis_at] // parts).reshape((-1,) + (1,) * (len(dims) - 1 - axis_at))
    return gain


def cumulative_ranks(number_of, slope):
    portions = [(1 << 20) // math.isqrt(standing ** slope) + 1 for standing in range(1, number_of + 1)]
    spread = 1 + sum(portions) // (1 << 30)
    return np.cumsum(np.array([max(1, weight // spread) for weight in portions]))


def ranked(key, shape, number_of, slope):
    table = cumulative_ranks(number_of, slope)
    lot = jax.random.randint(jax.random.fold_in(key, 1), shape, 0, int(table[number_of - 1]))
    rank = jnp.searchsorted(jnp.asarray(table, jnp.int32), lot, side="right")
    return jax.random.permutation(jax.random.fold_in(key, 2), number_of)[rank].astype(jnp.int32)


def bell_draw(stream_key, extent, deviation, limit, shards=(), held_as=jnp.bfloat16):
    drawn = deviation * jax.random.normal(stream_key, extent, jnp.float32)
    if shards:
        drawn = drawn * level_of(stream_key, extent, shards, -0.22, 0.18)
    return jnp.clip(drawn, -limit, limit).astype(held_as)


def bell_draw_with(own_key, shape, deviation, limit, shards, heavy, held_as=jnp.bfloat16):
    result = deviation * jax.random.normal(own_key, shape, jnp.float32)
    if shards:
        result = result * level_of(own_key, shape, shards, -0.22, 0.18)
    return jnp.clip(raised(result, jax.random.fold_in(own_key, 3), *heavy), -limit, limit).astype(held_as)


def setup_inputs(seed: int = 0) -> dict:
    keys = jax.random.split(jax.random.key(seed), 10)
    top_grad = bell_draw(keys[0], (BATCH, GROUPS, COMP), 1.0, 6.0, ((0, 1024),))
    pooled_in = bell_draw_with(keys[1], (GROUPS, BATCH, WIDTH), 1.0, 6.0, ((0, 64), (1, 16)), (1, 2, 16, 2.0))
    w_down = bell_draw(keys[2], (GROUPS, WIDTH, RANK), WIDTH ** -0.5, 0.125, ((0, 64),))
    w_up = bell_draw(keys[3], (GROUPS, RANK, WIDTH), RANK ** -0.5, 0.375, ((0, 64),))
    cross_bias = bell_draw(keys[4], (GROUPS, WIDTH), 0.5, 3.0, ((0, 64),), jnp.float32)
    w_comp = bell_draw(keys[5], (GROUPS, WIDTH, COMP), COMP ** -0.5, 0.375, ((0, 64),))
    feature_slot = jax.vmap(lambda own: jax.random.permutation(own, FEATS))(jax.random.split(keys[6], GROUPS)).reshape((GROUPS, FEATS)).astype(jnp.int32)
    bag_ids = place_ends(ranked(keys[7], (GROUPS, FEATS, BATCH, SLOTS), TABLE_ROWS, 2), jax.random.fold_in(keys[7], 3), 0, TABLE_ROWS - 1).astype(jnp.int32)
    bag_lengths = place_ends(jax.random.randint(keys[8], (GROUPS, FEATS, BATCH), 1, SLOTS + 1), jax.random.fold_in(keys[8], 1), 1, SLOTS).astype(jnp.int32)
    return dict(top_grad=top_grad, pooled_in=pooled_in, w_down=w_down, w_up=w_up, cross_bias=cross_bias, w_comp=w_comp, feature_slot=feature_slot, bag_ids=bag_ids, bag_lengths=bag_lengths)


def contract_rows(left, right):
    return lax.dot_general(left, right, (((0,), (0,)), ((), ())), preferred_element_type=jnp.float32)


def bag_tables(input_grad, slot_order, bag_ids, bag_lengths):
    rows_all = input_grad.shape[0]
    by_table = jnp.take(input_grad.reshape(rows_all, FEATS, EMBED), slot_order, axis=1)
    slot_index = jnp.arange(SLOTS, dtype=jnp.int32)

    def one_table(item):
        table_rows, table_ids, table_lengths = item
        inverse = 1.0 / table_lengths.astype(jnp.float32)
        weights = jnp.where(slot_index[None, :] < table_lengths[:, None], inverse[:, None], jnp.zeros_like(inverse)[:, None])
        values = weights[:, :, None] * table_rows.astype(jnp.float32)[:, None, :]
        return jax.ops.segment_sum(values.reshape(-1, EMBED), table_ids.reshape(-1), num_segments=TABLE_ROWS)

    return lax.map(one_table, (jnp.swapaxes(by_table, 0, 1), bag_ids, bag_lengths))


def one_group(item):
    out_grad, inputs, w_down, w_up, cross_bias, w_comp, feature_slot, bag_ids, bag_lengths = item
    low_rank = jnp.dot(inputs, w_down, preferred_element_type=jnp.float32).astype(jnp.bfloat16)
    scale_pre = jnp.dot(low_rank, w_up, preferred_element_type=jnp.float32) + cross_bias
    crossed = (inputs.astype(jnp.float32) * scale_pre + inputs.astype(jnp.float32)).astype(jnp.bfloat16)
    cross_grad = jnp.dot(out_grad, w_comp.T, preferred_element_type=jnp.float32)
    grad_comp = contract_rows(crossed, out_grad)
    scale_grad = (cross_grad * inputs.astype(jnp.float32)).astype(jnp.bfloat16)
    grad_up = contract_rows(low_rank, scale_grad)
    grad_bias = jnp.sum(scale_grad.astype(jnp.float32), axis=0)
    rank_grad = jnp.dot(scale_grad, w_up.T, preferred_element_type=jnp.float32).astype(jnp.bfloat16)
    grad_down = contract_rows(inputs, rank_grad)
    back_term = jnp.dot(rank_grad, w_down.T, preferred_element_type=jnp.float32)
    input_grad = (cross_grad * (scale_pre + 1.0) + back_term).astype(jnp.bfloat16)
    slot_order = jnp.argsort(feature_slot).astype(jnp.int32)
    tables = bag_tables(input_grad, slot_order, bag_ids, bag_lengths)
    return grad_down, grad_up, grad_bias, grad_comp, tables


def reference(top_grad, pooled_in, w_down, w_up, cross_bias, w_comp, feature_slot, bag_ids, bag_lengths):
    per_group = jnp.swapaxes(top_grad, 0, 1)
    grad_down, grad_up, grad_bias, grad_comp, table_grads = lax.map(
        one_group, (per_group, pooled_in, w_down, w_up, cross_bias, w_comp, feature_slot, bag_ids, bag_lengths))
    return (grad_down, grad_up, grad_bias, grad_comp, table_grads)
```

```python
import functools

import jax
import jax.numpy as jnp
from jax import lax
from jax.experimental import pallas as pl
from jax.experimental.pallas import tpu as pltpu
from jax.sharding import PartitionSpec as P

EMBED = 128
COMP = 256
RANK = 256
TABLE_ROWS = 512
SLOTS = 8
CHIPS = 8
CORES = 2
BLOCK = 128
HALF = CHIPS * BLOCK

SAME_CORE = [[chip * CORES + core for chip in range(CHIPS)] for core in range(CORES)]
SWAP = [(t, t ^ 1) for t in range(CHIPS * CORES)]


def shifted(step):
    return [
        (chip * CORES + core, (chip + step) % CHIPS * CORES + core)
        for chip in range(CHIPS)
        for core in range(CORES)
    ]


def contract_rows(left, right):
    return lax.dot_general(
        left, right, (((0,), (0,)), ((), ())), preferred_element_type=jnp.float32
    )


def contract_cols(left, right):
    return lax.dot_general(
        left, right, (((1,), (1,)), ((), ())), preferred_element_type=jnp.float32
    )


def product(left, right):
    return jnp.dot(left, right, preferred_element_type=jnp.float32)


def counts_kernel(ids_ref, lengths_ref, counts_ref):
    tile = counts_ref.shape[0]
    first = pl.program_id(0) * tile
    lengths = lengths_ref[...]
    row_values = first + lax.broadcasted_iota(jnp.int32, counts_ref.shape, 0)
    total = jnp.zeros(counts_ref.shape, jnp.float32)
    for slot in range(SLOTS):
        live = jnp.where(lengths > slot, ids_ref[slot : slot + 1, :], -1)
        total = total + jnp.where(live == row_values, 1.0, 0.0)
    counts_ref[...] = total.astype(jnp.bfloat16)


def bag_counts(ids, lengths):
    bags = ids.shape[1]
    tile = 64
    return pl.pallas_call(
        counts_kernel,
        grid=(TABLE_ROWS // tile,),
        in_specs=[
            pl.BlockSpec((SLOTS, bags), lambda i: (0, 0)),
            pl.BlockSpec((1, bags), lambda i: (0, 0)),
        ],
        out_specs=pl.BlockSpec((tile, bags), lambda i: (i, 0)),
        out_shape=jax.ShapeDtypeStruct((TABLE_ROWS, bags), jnp.bfloat16),
        cost_estimate=pl.CostEstimate(
            flops=30_000_000_00, bytes_accessed=3_000_000, transcendentals=0
        ),
        name="bag_counts",
    )(ids, lengths)


def half_kernel(
    first,
    place_ref,
    grads_ref,
    saved_ref,
    counts_ref,
    inverse_ref,
    comp_ref,
    up_ref,
    bias_ref,
    down_ref,
    *refs,
):
    if first:
        before = (None,) * 5
    else:
        before, refs = refs[:5], refs[5:]
    out_refs, (crossed_ref, scale_ref, split_ref, low_flat, x_flat, counts_flat) = refs[:5], refs[5:]
    core = place_ref[0]
    chip = place_ref[1]
    if not first:
        core = 1 - core

    @pl.loop(0, CHIPS)
    def _(k):
        rows = pl.ds(pl.multiple_of(k * BLOCK, BLOCK), BLOCK)
        block = k * CORES + core
        at = lax.rem(chip - k + CHIPS, CHIPS)
        x = saved_ref[at, 0]
        low = jnp.concatenate(
            [saved_ref[at, saved_ref.shape[1] - 2], saved_ref[at, saved_ref.shape[1] - 1]], axis=1
        )
        low_flat[rows, :] = low
        x_flat[rows, :] = x
        out_grad = grads_ref[rows, :COMP]
        rank_grad = grads_ref[rows, COMP:]
        cross = contract_cols(out_grad, comp_ref[...])
        scale = product(low, up_ref[...]) + bias_ref[...]
        back = contract_cols(rank_grad, down_ref[...])
        input_grad = (cross[:, EMBED:] * (scale[:, EMBED:] + 1.0) + back).astype(jnp.bfloat16)
        scaled = input_grad.astype(jnp.float32) * inverse_ref[block]
        high = scaled.astype(jnp.bfloat16)
        split_ref[rows, :EMBED] = high
        split_ref[rows, EMBED:] = (scaled - high.astype(jnp.float32)).astype(jnp.bfloat16)
        wide = x.astype(jnp.float32)
        crossed_ref[rows, :] = (wide * scale[:, :EMBED] + wide).astype(jnp.bfloat16)
        scale_ref[rows, :] = (cross[:, :EMBED] * wide).astype(jnp.bfloat16)
        counts_flat[:, rows] = counts_ref[
            :, pl.ds(pl.multiple_of(block * BLOCK, BLOCK), BLOCK)
        ]

    table = product(counts_flat[...], split_ref[...])
    terms = [
        contract_rows(x_flat[...], grads_ref[:, COMP:]),
        contract_rows(scale_ref[...], low_flat[...]),
        jnp.sum(scale_ref[...].astype(jnp.float32), axis=0, keepdims=True),
        contract_rows(crossed_ref[...], grads_ref[:, :COMP]),
        table[:, :EMBED] + table[:, EMBED:],
    ]
    if not first:
        terms = [term + ref[...] for term, ref in zip(terms, before)]
        terms[1] = terms[1].T
    for ref, term in zip(out_refs, terms):
        ref[...] = term


def half(place, grads, saved, counts, inverse, weights, before=None):
    first = before is None
    shapes = [(EMBED, RANK), (EMBED, RANK), (1, EMBED), (EMBED, COMP), (TABLE_ROWS, EMBED)]
    if not first:
        shapes[1] = (RANK, EMBED)
    whole = pl.BlockSpec(memory_space=pltpu.VMEM)
    operands = [grads, saved, counts, inverse, *weights] + ([] if first else list(before))
    return pl.pallas_call(
        functools.partial(half_kernel, first),
        in_specs=[pl.BlockSpec(memory_space=pltpu.SMEM)] + [whole] * len(operands),
        out_specs=[whole] * 5,
        out_shape=[jax.ShapeDtypeStruct(shape, jnp.float32) for shape in shapes],
        scratch_shapes=[
            pltpu.VMEM((HALF, EMBED), jnp.bfloat16),
            pltpu.VMEM((HALF, EMBED), jnp.bfloat16),
            pltpu.VMEM((HALF, 2 * EMBED), jnp.bfloat16),
            pltpu.VMEM((HALF, RANK), jnp.bfloat16),
            pltpu.VMEM((HALF, EMBED), jnp.bfloat16),
            pltpu.VMEM((TABLE_ROWS, HALF), jnp.bfloat16),
        ],
        compiler_params=pltpu.CompilerParams(vmem_limit_bytes=32 * 1024 * 1024),
        cost_estimate=pl.CostEstimate(
            flops=1_500_000_000, bytes_accessed=6_000_000, transcendentals=0
        ),
        name="column_half_first" if first else "column_half_second",
    )(place, *operands)


def pack_kernel(place_ref, x_ref, down_ref, blocks_ref):
    core, chip = place_ref[0], place_ref[1]
    low = product(x_ref[...], down_ref[...]).astype(jnp.bfloat16)
    for step in range(CHIPS):
        base = lax.rem(chip + step, CHIPS) * CORES
        for turn in range(CORES):
            slot = base + (core if turn == 0 else 1 - core)
            blocks_ref[step, turn] = x_ref[:, pl.ds(pl.multiple_of(slot * EMBED, EMBED), EMBED)]
        blocks_ref[step, 2] = low[:, :BLOCK]
        blocks_ref[step, 3] = low[:, BLOCK:]


def pack(place, inputs, down_mat):
    whole = pl.BlockSpec(memory_space=pltpu.VMEM)
    return pl.pallas_call(
        pack_kernel,
        in_specs=[pl.BlockSpec(memory_space=pltpu.SMEM), whole, whole],
        out_specs=whole,
        out_shape=jax.ShapeDtypeStruct((CHIPS, 4, BLOCK, EMBED), jnp.bfloat16),
        compiler_params=pltpu.CompilerParams(vmem_limit_bytes=16 * 1024 * 1024),
        cost_estimate=pl.CostEstimate(
            flops=140_000_000, bytes_accessed=2_600_000, transcendentals=0
        ),
        name="low_rank_and_columns",
    )(place, inputs, down_mat)


def on_device(
    top_grad, pooled_in, w_down, w_up, cross_bias, w_comp, feature_slot, bag_ids, bag_lengths
):
    arrived = lax.all_to_all(top_grad, "hst", split_axis=1, concat_axis=0, tiled=True)
    out_grad = arrived.reshape(BLOCK, COMP)
    me = lax.axis_index("tower")
    place = jnp.stack([me & 1, me >> 1]).astype(jnp.int32)
    inputs, down_mat, up_mat, comp_mat = pooled_in[0], w_down[0], w_up[0], w_comp[0]

    packed = pack(place, inputs, down_mat)
    arrived_blocks = [packed[0]] + [
        lax.ppermute(packed[step], "tower", shifted(step)) for step in range(1, CHIPS)
    ]

    counts = bag_counts(jnp.transpose(bag_ids[0, 0]), bag_lengths[0])
    inverse = jnp.broadcast_to(
        (1.0 / bag_lengths[0, 0].astype(jnp.float32))[:, None], (CHIPS * CORES * BLOCK, EMBED)
    ).reshape(CHIPS * CORES, BLOCK, EMBED)
    slot = jnp.sum(jnp.where(feature_slot[0] == me, jnp.arange(CHIPS * CORES, dtype=jnp.int32), 0))

    def two_slots(array, axis):
        return jnp.concatenate(
            [
                lax.dynamic_slice_in_dim(array, me * EMBED, EMBED, axis),
                lax.dynamic_slice_in_dim(array, slot * EMBED, EMBED, axis),
            ],
            axis,
        )

    weights = (
        two_slots(comp_mat, 0),
        two_slots(up_mat, 1),
        two_slots(cross_bias, 1),
        lax.dynamic_slice_in_dim(down_mat, slot * EMBED, EMBED, 0),
    )

    cross_grad = contract_cols(out_grad, comp_mat)
    scale_grad = (cross_grad * inputs.astype(jnp.float32)).astype(jnp.bfloat16)
    rank_grad = contract_cols(scale_grad, up_mat).astype(jnp.bfloat16)

    both = jnp.concatenate([out_grad, rank_grad], axis=1)
    both, *arrived_blocks = lax.optimization_barrier((both, *arrived_blocks))
    own = jnp.stack(arrived_blocks)
    other = lax.ppermute(own[:, 1:], "tower", SWAP)
    grads_own = lax.all_to_all(
        jnp.broadcast_to(both[None], (CHIPS, BLOCK, COMP + RANK)),
        "tower",
        split_axis=0,
        concat_axis=0,
        tiled=True,
        axis_index_groups=SAME_CORE,
    ).reshape(HALF, COMP + RANK)
    grads_other = lax.ppermute(grads_own, "tower", SWAP)

    first = half(place, grads_own, own, counts, inverse, weights)
    grad_down, grad_up, grad_bias, grad_comp, tables = half(
        place, grads_other, other, counts, inverse, weights, first
    )
    return grad_down[None], grad_up[None], grad_bias, grad_comp[None], tables[None, None]


def solution(mesh):
    placed = (
        P(("tower", "hst"), None, None),
        P("hst", "tower", None),
        P("hst", None, None),
        P("hst", None, None),
        P("hst", None),
        P("hst", None, None),
        P("hst", None),
        P("hst", "tower", None, None),
        P("hst", "tower", None),
    )
    return jax.shard_map(
        on_device,
        mesh=mesh,
        in_specs=placed,
        out_specs=(
            P("hst", "tower", None),
            P("hst", None, "tower"),
            P("hst", "tower"),
            P("hst", "tower", None),
            P("hst", "tower", None, None),
        ),
        check_vma=False,
    )
```

```python
import functools

import jax
import jax.numpy as jnp
from jax import lax
from jax.experimental import pallas as pl
from jax.experimental.pallas import tpu as pltpu
from jax.sharding import PartitionSpec as P

EMBED = 128
COMP = 256
RANK = 256
TABLE_ROWS = 512
SLOTS = 8
CHIPS = 8
CORES = 2
BLOCK = 128
HALF = CHIPS * BLOCK

PACK_FLOPS = 270_000_000
RANK_FLOPS = 270_000_000

NEAR = CHIPS // 2 - 1
SAME_CORE = [[chip * CORES + core for chip in range(CHIPS)] for core in range(CORES)]
SWAP = [(t, t ^ 1) for t in range(CHIPS * CORES)]


def both_ways(step):
    pairs = []
    for chip in range(CHIPS):
        pairs.append((chip * CORES, (chip + step) % CHIPS * CORES))
        pairs.append((chip * CORES + 1, (chip - step) % CHIPS * CORES + 1))
    return pairs


def contract_rows(left, right):
    return lax.dot_general(
        left, right, (((0,), (0,)), ((), ())), preferred_element_type=jnp.float32
    )


def contract_cols(left, right):
    return lax.dot_general(
        left, right, (((1,), (1,)), ((), ())), preferred_element_type=jnp.float32
    )


def product(left, right):
    return jnp.dot(left, right, preferred_element_type=jnp.float32)


def counts_kernel(ids_ref, lengths_ref, counts_ref):
    tile = counts_ref.shape[0]
    first = pl.program_id(0) * tile
    lengths = lengths_ref[...]
    row_values = first + lax.broadcasted_iota(jnp.int32, counts_ref.shape, 0)
    total = jnp.zeros(counts_ref.shape, jnp.float32)
    for slot in range(SLOTS):
        live = jnp.where(lengths > slot, ids_ref[slot : slot + 1, :], -1)
        total = total + jnp.where(live == row_values, 1.0, 0.0)
    counts_ref[...] = total.astype(jnp.bfloat16)


def bag_counts(ids, lengths):
    bags = ids.shape[1]
    tile = 64
    return pl.pallas_call(
        counts_kernel,
        grid=(TABLE_ROWS // tile,),
        in_specs=[
            pl.BlockSpec((SLOTS, bags), lambda i: (0, 0)),
            pl.BlockSpec((1, bags), lambda i: (0, 0)),
        ],
        out_specs=pl.BlockSpec((tile, bags), lambda i: (i, 0)),
        out_shape=jax.ShapeDtypeStruct((TABLE_ROWS, bags), jnp.bfloat16),
        cost_estimate=pl.CostEstimate(
            flops=30_000_000_00, bytes_accessed=3_000_000, transcendentals=0
        ),
        name="bag_counts",
    )(ids, lengths)


def half_kernel(
    first,
    place_ref,
    grads_ref,
    keep_ref,
    taken_ref,
    counts_ref,
    inverse_ref,
    comp_ref,
    up_ref,
    bias_ref,
    down_ref,
    *refs,
):
    if first:
        before = (None,) * 5
    else:
        before, refs = refs[:5], refs[5:]
    out_refs, (crossed_ref, scale_ref, split_ref, low_flat, x_flat, counts_flat) = refs[:5], refs[5:]
    mine, chip = place_ref[0], place_ref[1]
    core = mine if first else 1 - mine

    @pl.loop(0, CHIPS)
    def _(k):
        rows = pl.ds(pl.multiple_of(k * BLOCK, BLOCK), BLOCK)
        block = k * CORES + core
        way = lax.rem((chip - k) * (1 - 2 * mine) + CHIPS, CHIPS)
        given = (way > CHIPS // 2) | ((lax.rem(way, CHIPS // 2) == 0) & (core != mine))
        near = jnp.where(way > CHIPS // 2, CHIPS - way, way)
        holder = jnp.where(given, 1 - mine, mine)
        inner = 2 * near - 1 + jnp.where(core == holder, 0, 1)
        at = jnp.where(near == 0, 0, jnp.where(near == CHIPS // 2, CHIPS - 1, inner))

        @pl.when(given)
        def _():
            x_flat[rows, :] = taken_ref[at, 2]
            low_flat[rows, :BLOCK] = taken_ref[at, 0]
            low_flat[rows, BLOCK:] = taken_ref[at, 1]

        @pl.when(jnp.logical_not(given))
        def _():
            x_flat[rows, :] = keep_ref[at, 0]
            low_flat[rows, :BLOCK] = keep_ref[at, 1]
            low_flat[rows, BLOCK:] = keep_ref[at, 2]

        x = x_flat[rows, :]
        low = low_flat[rows, :]
        out_grad = grads_ref[rows, :COMP]
        rank_grad = grads_ref[rows, COMP:]
        cross = contract_cols(out_grad, comp_ref[...])
        scale = product(low, up_ref[...]) + bias_ref[...]
        back = contract_cols(rank_grad, down_ref[...])
        input_grad = (cross[:, EMBED:] * (scale[:, EMBED:] + 1.0) + back).astype(jnp.bfloat16)
        scaled = input_grad.astype(jnp.float32) * inverse_ref[block]
        high = scaled.astype(jnp.bfloat16)
        split_ref[rows, :EMBED] = high
        split_ref[rows, EMBED:] = (scaled - high.astype(jnp.float32)).astype(jnp.bfloat16)
        wide = x.astype(jnp.float32)
        crossed_ref[rows, :] = (wide * scale[:, :EMBED] + wide).astype(jnp.bfloat16)
        scale_ref[rows, :] = (cross[:, :EMBED] * wide).astype(jnp.bfloat16)
        counts_flat[:, rows] = counts_ref[
            :, pl.ds(pl.multiple_of(block * BLOCK, BLOCK), BLOCK)
        ]

    table = product(counts_flat[...], split_ref[...])
    terms = [
        contract_rows(x_flat[...], grads_ref[:, COMP:]),
        contract_rows(scale_ref[...], low_flat[...]),
        jnp.sum(scale_ref[...].astype(jnp.float32), axis=0, keepdims=True),
        contract_rows(crossed_ref[...], grads_ref[:, :COMP]),
        table[:, :EMBED] + table[:, EMBED:],
    ]
    if not first:
        terms = [term + ref[...] for term, ref in zip(terms, before)]
        terms[1] = terms[1].T
    for ref, term in zip(out_refs, terms):
        ref[...] = term


def half(place, grads, keep, taken, counts, inverse, weights, before=None):
    first = before is None
    shapes = [(EMBED, RANK), (EMBED, RANK), (1, EMBED), (EMBED, COMP), (TABLE_ROWS, EMBED)]
    if not first:
        shapes[1] = (RANK, EMBED)
    operands = [grads, keep, taken, counts, inverse, *weights] + ([] if first else list(before))
    return pl.pallas_call(
        functools.partial(half_kernel, first),
        in_specs=[SCALARS] + [WHOLE] * len(operands),
        out_specs=[WHOLE] * 5,
        out_shape=[jax.ShapeDtypeStruct(shape, jnp.float32) for shape in shapes],
        scratch_shapes=[
            pltpu.VMEM((HALF, EMBED), jnp.bfloat16),
            pltpu.VMEM((HALF, EMBED), jnp.bfloat16),
            pltpu.VMEM((HALF, 2 * EMBED), jnp.bfloat16),
            pltpu.VMEM((HALF, RANK), jnp.bfloat16),
            pltpu.VMEM((HALF, EMBED), jnp.bfloat16),
            pltpu.VMEM((TABLE_ROWS, HALF), jnp.bfloat16),
        ],
        compiler_params=pltpu.CompilerParams(vmem_limit_bytes=32 * 1024 * 1024),
        cost_estimate=pl.CostEstimate(
            flops=1_500_000_000, bytes_accessed=6_000_000, transcendentals=0
        ),
        name="column_half_first" if first else "column_half_second",
    )(place, *operands)


def pack_kernel(place_ref, x_ref, partner_ref, down_ref, self_ref, near_ref, far_ref):
    core, chip = place_ref[0], place_ref[1]
    way = 1 - 2 * core
    sides = []
    for ref in (x_ref, partner_ref):
        low = product(ref[...], down_ref[...]).astype(jnp.bfloat16)
        sides.append((ref, low))

    def fill(step, side, put):
        ref, low = sides[side]
        base = lax.rem(chip + way * step + CHIPS, CHIPS) * CORES
        for part, slot in ((0, base + core), (3, base + 1 - core)):
            put(part, ref[:, pl.ds(pl.multiple_of(slot * EMBED, EMBED), EMBED)])
        put(1, low[:, :BLOCK])
        put(2, low[:, BLOCK:])

    def put_self(part, value):
        self_ref[part] = value

    def put_far(part, value):
        far_ref[part] = value

    fill(0, 0, put_self)
    fill(CHIPS // 2, 0, put_far)
    for step in range(1, NEAR + 1):
        for side in range(2):

            def put_near(part, value, step=step, side=side):
                near_ref[step - 1, side, part] = value

            fill(step, side, put_near)


WHOLE = pl.BlockSpec(memory_space=pltpu.VMEM)
SCALARS = pl.BlockSpec(memory_space=pltpu.SMEM)


def pack(place, inputs, partner, down_mat):
    tile = (4, BLOCK, EMBED)
    return pl.pallas_call(
        pack_kernel,
        in_specs=[SCALARS, WHOLE, WHOLE, WHOLE],
        out_specs=[WHOLE] * 3,
        out_shape=[
            jax.ShapeDtypeStruct(tile, jnp.bfloat16),
            jax.ShapeDtypeStruct((NEAR, 2, *tile), jnp.bfloat16),
            jax.ShapeDtypeStruct(tile, jnp.bfloat16),
        ],
        compiler_params=pltpu.CompilerParams(vmem_limit_bytes=16 * 1024 * 1024),
        cost_estimate=pl.CostEstimate(
            flops=PACK_FLOPS, bytes_accessed=3_000_000, transcendentals=0
        ),
        name="low_rank_and_columns",
    )(place, inputs, partner, down_mat)


def merge_kernel(self_ref, first_ref, second_ref, third_ref, far_ref, keep_ref, give_ref):
    blocks = [self_ref]
    for ref in (first_ref, second_ref, third_ref):
        blocks += [ref.at[0], ref.at[1]]
    blocks.append(far_ref)
    for index, block in enumerate(blocks):
        keep_ref[index] = block[0:3]
        give_ref[index] = block[1:4]


def merge(blocks):
    shape = jax.ShapeDtypeStruct((CHIPS, 3, BLOCK, EMBED), jnp.bfloat16)
    return pl.pallas_call(
        merge_kernel,
        in_specs=[WHOLE] * 5,
        out_specs=[WHOLE] * 2,
        out_shape=[shape, shape],
        compiler_params=pltpu.CompilerParams(vmem_limit_bytes=16 * 1024 * 1024),
        cost_estimate=pl.CostEstimate(flops=0, bytes_accessed=3_000_000, transcendentals=0),
        name="merge_rows",
    )(*blocks)


def rank_kernel(grad_ref, x_ref, comp_ref, up_ref, out_ref):
    out_grad = grad_ref[...]
    total = jnp.zeros((BLOCK, RANK), jnp.float32)
    width = 512
    for start in range(0, x_ref.shape[1], width):
        columns = pl.ds(start, width)
        cross = contract_cols(out_grad, comp_ref[columns, :])
        scale_grad = (cross * x_ref[:, columns].astype(jnp.float32)).astype(jnp.bfloat16)
        total += contract_cols(scale_grad, up_ref[:, columns])
    rank_grad = total.astype(jnp.bfloat16)
    for chip in range(CHIPS):
        out_ref[chip, :, :COMP] = out_grad
        out_ref[chip, :, COMP:] = rank_grad


def rank_rows(out_grad, inputs, comp_mat, up_mat):
    return pl.pallas_call(
        rank_kernel,
        in_specs=[WHOLE] * 4,
        out_specs=WHOLE,
        out_shape=jax.ShapeDtypeStruct((CHIPS, BLOCK, COMP + RANK), jnp.bfloat16),
        compiler_params=pltpu.CompilerParams(vmem_limit_bytes=16 * 1024 * 1024),
        cost_estimate=pl.CostEstimate(
            flops=RANK_FLOPS, bytes_accessed=3_600_000, transcendentals=0
        ),
        name="rank_grad_rows",
    )(out_grad, inputs, comp_mat, up_mat)


def on_device(
    top_grad, pooled_in, w_down, w_up, cross_bias, w_comp, feature_slot, bag_ids, bag_lengths
):
    arrived = lax.all_to_all(top_grad, "hst", split_axis=1, concat_axis=0, tiled=True)
    out_grad = arrived.reshape(BLOCK, COMP)
    me = lax.axis_index("tower")
    place = jnp.stack([me & 1, me >> 1]).astype(jnp.int32)
    inputs, down_mat, up_mat, comp_mat = pooled_in[0], w_down[0], w_up[0], w_comp[0]

    partner = lax.ppermute(inputs, "tower", SWAP)
    blocks, near, far = pack(place, inputs, partner, down_mat)
    received = [
        lax.ppermute(near[step - 1], "tower", both_ways(step)) for step in range(1, NEAR + 1)
    ]
    received.append(lax.ppermute(far, "tower", both_ways(CHIPS // 2)))

    counts = bag_counts(jnp.transpose(bag_ids[0, 0]), bag_lengths[0])
    inverse = jnp.broadcast_to(
        (1.0 / bag_lengths[0, 0].astype(jnp.float32))[:, None], (CHIPS * CORES * BLOCK, EMBED)
    ).reshape(CHIPS * CORES, BLOCK, EMBED)
    slot = jnp.sum(jnp.where(feature_slot[0] == me, jnp.arange(CHIPS * CORES, dtype=jnp.int32), 0))

    def two_slots(array, axis):
        return jnp.concatenate(
            [
                lax.dynamic_slice_in_dim(array, me * EMBED, EMBED, axis),
                lax.dynamic_slice_in_dim(array, slot * EMBED, EMBED, axis),
            ],
            axis,
        )

    weights = (
        two_slots(comp_mat, 0),
        two_slots(up_mat, 1),
        two_slots(cross_bias, 1),
        lax.dynamic_slice_in_dim(down_mat, slot * EMBED, EMBED, 0),
    )

    rows_out = rank_rows(out_grad, inputs, comp_mat, up_mat)
    rows_out, *received = lax.optimization_barrier((rows_out, *received))
    keep, give = merge([blocks, *received])
    taken = lax.ppermute(give, "tower", SWAP)
    grads_own = lax.all_to_all(
        rows_out,
        "tower",
        split_axis=0,
        concat_axis=0,
        tiled=True,
        axis_index_groups=SAME_CORE,
    ).reshape(HALF, COMP + RANK)
    grads_other = lax.ppermute(grads_own, "tower", SWAP)

    first = half(place, grads_own, keep, taken, counts, inverse, weights)
    grad_down, grad_up, grad_bias, grad_comp, tables = half(
        place, grads_other, keep, taken, counts, inverse, weights, first
    )
    return grad_down[None], grad_up[None], grad_bias, grad_comp[None], tables[None, None]


def solution(mesh):
    placed = (
        P(("tower", "hst"), None, None),
        P("hst", "tower", None),
        P("hst", None, None),
        P("hst", None, None),
        P("hst", None),
        P("hst", None, None),
        P("hst", None),
        P("hst", "tower", None, None),
        P("hst", "tower", None),
    )
    return jax.shard_map(
        on_device,
        mesh=mesh,
        in_specs=placed,
        out_specs=(
            P("hst", "tower", None),
            P("hst", None, "tower"),
            P("hst", "tower"),
            P("hst", "tower", None),
            P("hst", "tower", None, None),
        ),
        check_vma=False,
    )
```

```python
import jax
import jax.numpy as jnp
from jax import lax
from jax.experimental import pallas as pl
from jax.experimental.pallas import tpu as pltpu
from jax.sharding import PartitionSpec as P

EMBED = 128
COMP = 256
RANK = 256
TABLE_ROWS = 512
SLOTS = 8
CHIPS = 8
CORES = 2
BLOCK = 128
HALF = CHIPS * BLOCK

STEPS = 4
ROOM = 60 * 1024 * 1024
PACK_FLOPS = 270_000_000
RANK_FLOPS = 270_000_000

NEAR = CHIPS // 2 - 1
SAME_CORE = [[chip * CORES + core for chip in range(CHIPS)] for core in range(CORES)]
SWAP = [(t, t ^ 1) for t in range(CHIPS * CORES)]


def both_ways(step):
    pairs = []
    for chip in range(CHIPS):
        pairs.append((chip * CORES, (chip + step) % CHIPS * CORES))
        pairs.append((chip * CORES + 1, (chip - step) % CHIPS * CORES + 1))
    return pairs


def contract_rows(left, right):
    return lax.dot_general(
        left, right, (((0,), (0,)), ((), ())), preferred_element_type=jnp.float32
    )


def contract_cols(left, right):
    return lax.dot_general(
        left, right, (((1,), (1,)), ((), ())), preferred_element_type=jnp.float32
    )


def product(left, right):
    return jnp.dot(left, right, preferred_element_type=jnp.float32)


def half_kernel(*refs):
    grads_ref, low_ref, x_ref, crossed_ref, scale_ref, counts_ref, spread_ref, comp_ref, down_ref = (
        refs[:9]
    )
    before, out_refs = refs[9:-5], refs[-5:]

    @pl.when(pl.program_id(0) == 0)
    def _():
        for index, ref in enumerate(out_refs):
            ref[...] = before[index][...] if before else jnp.zeros(ref.shape, ref.dtype)

    out_grad = grads_ref[:, :COMP]
    rank_grad = grads_ref[:, COMP:]
    x = x_ref[0]
    cross = contract_cols(out_grad, comp_ref[...])
    back = contract_cols(rank_grad, down_ref[...])
    input_grad = (cross[:, EMBED:] * scale_ref[0] + back).astype(jnp.bfloat16)
    scaled = input_grad.astype(jnp.float32) * spread_ref[0]
    high = scaled.astype(jnp.bfloat16)
    rest = (scaled - high.astype(jnp.float32)).astype(jnp.bfloat16)
    table = product(counts_ref[0], jnp.concatenate([high, rest], axis=1))
    scale_grad = (cross[:, :EMBED] * x.astype(jnp.float32)).astype(jnp.bfloat16)
    down_out, up_out, bias_out, comp_out, table_out = out_refs
    down_out[...] += contract_rows(x, rank_grad)
    up_out[...] += contract_rows(low_ref[0], scale_grad)
    bias_out[...] += jnp.sum(scale_grad.astype(jnp.float32), axis=0, keepdims=True)
    comp_out[...] += contract_rows(crossed_ref[0], out_grad)
    table_out[...] += table[:, :EMBED] + table[:, EMBED:]


def half(side, grads, saved, before=()):
    step = HALF // STEPS
    shapes = [(EMBED, RANK), (RANK, EMBED), (1, EMBED), (EMBED, COMP), (TABLE_ROWS, EMBED)]

    def rows(width):
        return pl.BlockSpec((1, step, width), lambda i: (side, i, 0))

    in_specs = [
        pl.BlockSpec((step, COMP + RANK), lambda i: (i, 0)),
        rows(RANK),
        rows(EMBED),
        rows(EMBED),
        rows(EMBED),
        pl.BlockSpec((1, TABLE_ROWS, step), lambda i: (side, 0, i)),
        rows(EMBED),
        fetched((2 * EMBED, COMP)),
        fetched((EMBED, RANK)),
    ] + [fetched(array.shape) for array in before]
    return pl.pallas_call(
        half_kernel,
        grid=(STEPS,),
        in_specs=in_specs,
        out_specs=[fetched(shape) for shape in shapes],
        out_shape=[full_type(*shape) for shape in shapes],
        compiler_params=pltpu.CompilerParams(vmem_limit_bytes=ROOM),
        cost_estimate=pl.CostEstimate(
            flops=1_500_000_000, bytes_accessed=6_000_000, transcendentals=0
        ),
        name="column_half_second" if before else "column_half_first",
    )(grads, *saved, *before)


def pack_kernel(
    place_ref, x_ref, partner_ref, down_ref, self_ref, first_ref, second_ref, third_ref, far_ref
):
    core, chip = place_ref[0], place_ref[1]
    way = 1 - 2 * core
    sides = []
    for ref in (x_ref, partner_ref):
        low = product(ref[...], down_ref[...]).astype(jnp.bfloat16)
        sides.append((ref, low))

    def fill(step, side, target):
        ref, low = sides[side]
        base = lax.rem(chip + way * step + CHIPS, CHIPS) * CORES
        for part, slot in ((0, base + core), (3, base + 1 - core)):
            target[part] = ref[:, pl.ds(pl.multiple_of(slot * EMBED, EMBED), EMBED)]
        target[1] = low[:, :BLOCK]
        target[2] = low[:, BLOCK:]

    for step, near_ref in enumerate((first_ref, second_ref, third_ref), 1):
        for side in range(2):
            fill(step, side, near_ref.at[side])
    fill(CHIPS // 2, 0, far_ref)
    fill(0, 0, self_ref)


WHOLE = pl.BlockSpec(memory_space=pltpu.VMEM)
SCALARS = pl.BlockSpec(memory_space=pltpu.SMEM)


def fetched(shape):
    return pl.BlockSpec(shape, lambda i: (0,) * len(shape))


def call(kernel, place, operands, shapes, name, flops=1000, moved=1000):
    return pl.pallas_call(
        kernel,
        grid=(1,),
        in_specs=[SCALARS] + [fetched(operand.shape) for operand in operands],
        out_specs=[fetched(shape.shape) for shape in shapes],
        out_shape=shapes,
        compiler_params=pltpu.CompilerParams(vmem_limit_bytes=ROOM),
        cost_estimate=pl.CostEstimate(flops=flops, bytes_accessed=moved, transcendentals=0),
        name=name,
    )(place, *operands)


def half_type(*shape):
    return jax.ShapeDtypeStruct(shape, jnp.bfloat16)


def full_type(*shape):
    return jax.ShapeDtypeStruct(shape, jnp.float32)


TILE = (4, BLOCK, EMBED)


def merge_kernel(
    place_ref, self_ref, first_ref, second_ref, third_ref, far_ref, keep_ref, give_ref
):
    blocks = [self_ref]
    for ref in (first_ref, second_ref, third_ref):
        blocks += [ref.at[0], ref.at[1]]
    blocks.append(far_ref)
    for index, block in enumerate(blocks):
        keep_ref[index] = block[0:3]
        give_ref[index] = block[1:4]


def counts_kernel(place_ref, ids_ref, lengths_ref, inverse_ref, counts_ref, spread_ref):
    mine = place_ref[0]
    tile = 64

    @pl.loop(0, CHIPS * CORES)
    def _(block):
        side = jnp.where(lax.rem(block, CORES) == mine, 0, 1)
        bags = pl.ds(pl.multiple_of(block * BLOCK, BLOCK), BLOCK)
        to = pl.ds(pl.multiple_of(lax.div(block, CORES) * BLOCK, BLOCK), BLOCK)
        lengths = lengths_ref[:, bags]
        live = [
            jnp.where(lengths > slot, ids_ref[slot : slot + 1, bags], -1) for slot in range(SLOTS)
        ]
        for start in range(0, TABLE_ROWS, tile):
            row_values = start + lax.broadcasted_iota(jnp.int32, (tile, BLOCK), 0)
            total = jnp.zeros((tile, BLOCK), jnp.float32)
            for slot in range(SLOTS):
                total = total + jnp.where(live[slot] == row_values, 1.0, 0.0)
            counts_ref[side, start : start + tile, to] = total.astype(jnp.bfloat16)
        spread_ref[side, to, :] = jnp.broadcast_to(inverse_ref[:, bags], (BLOCK, BLOCK)).T


def saved_kernel(
    place_ref,
    keep_ref,
    taken_ref,
    down_ref,
    up_ref,
    bias_ref,
    comp_ref,
    low_ref,
    x_ref,
    crossed_ref,
    scale_ref,
    comp_out,
    down_out,
):
    mine, chip, me, slot = place_ref[0], place_ref[1], place_ref[2], place_ref[3]
    own = pl.ds(pl.multiple_of(me * EMBED, EMBED), EMBED)
    served = pl.ds(pl.multiple_of(slot * EMBED, EMBED), EMBED)
    comp_out[:EMBED, :] = comp_ref[own, :]
    comp_out[EMBED:, :] = comp_ref[served, :]
    down_out[...] = down_ref[served, :]
    ups = jnp.concatenate([up_ref[:, own], up_ref[:, served]], axis=1)
    bias = jnp.concatenate([bias_ref[:, own], bias_ref[:, served]], axis=1)
    for side in range(CORES):
        core = mine if side == 0 else 1 - mine

        @pl.loop(0, CHIPS)
        def _(k):
            rows = pl.ds(pl.multiple_of(k * BLOCK, BLOCK), BLOCK)
            way = lax.rem((chip - k) * (1 - 2 * mine) + CHIPS, CHIPS)
            given = (way > CHIPS // 2) | ((lax.rem(way, CHIPS // 2) == 0) & (core != mine))
            near = jnp.where(way > CHIPS // 2, CHIPS - way, way)
            holder = jnp.where(given, 1 - mine, mine)
            inner = 2 * near - 1 + jnp.where(core == holder, 0, 1)
            at = jnp.where(near == 0, 0, jnp.where(near == CHIPS // 2, CHIPS - 1, inner))

            @pl.when(given)
            def _():
                x_ref[side, rows, :] = taken_ref[at, 2]
                low_ref[side, rows, :BLOCK] = taken_ref[at, 0]
                low_ref[side, rows, BLOCK:] = taken_ref[at, 1]

            @pl.when(jnp.logical_not(given))
            def _():
                x_ref[side, rows, :] = keep_ref[at, 0]
                low_ref[side, rows, :BLOCK] = keep_ref[at, 1]
                low_ref[side, rows, BLOCK:] = keep_ref[at, 2]

        scale = product(low_ref[side], ups) + bias
        wide = x_ref[side].astype(jnp.float32)
        crossed_ref[side] = (wide * scale[:, :EMBED] + wide).astype(jnp.bfloat16)
        scale_ref[side] = scale[:, EMBED:] + 1.0


def rank_kernel(grad_ref, x_ref, comp_ref, up_ref, out_ref):
    out_grad = grad_ref[...]
    total = jnp.zeros((BLOCK, RANK), jnp.float32)
    width = 512
    for start in range(0, x_ref.shape[1], width):
        columns = pl.ds(start, width)
        cross = contract_cols(out_grad, comp_ref[columns, :])
        scale_grad = (cross * x_ref[:, columns].astype(jnp.float32)).astype(jnp.bfloat16)
        total += contract_cols(scale_grad, up_ref[:, columns])
    rank_grad = total.astype(jnp.bfloat16)
    for chip in range(CHIPS):
        out_ref[chip, :, :COMP] = out_grad
        out_ref[chip, :, COMP:] = rank_grad


def rank_rows(out_grad, inputs, comp_mat, up_mat):
    return pl.pallas_call(
        rank_kernel,
        in_specs=[WHOLE] * 4,
        out_specs=WHOLE,
        out_shape=jax.ShapeDtypeStruct((CHIPS, BLOCK, COMP + RANK), jnp.bfloat16),
        compiler_params=pltpu.CompilerParams(vmem_limit_bytes=16 * 1024 * 1024),
        cost_estimate=pl.CostEstimate(
            flops=RANK_FLOPS, bytes_accessed=3_600_000, transcendentals=0
        ),
        name="rank_grad_rows",
    )(out_grad, inputs, comp_mat, up_mat)


def on_device(
    top_grad, pooled_in, w_down, w_up, cross_bias, w_comp, feature_slot, bag_ids, bag_lengths
):
    arrived = lax.all_to_all(top_grad, "hst", split_axis=1, concat_axis=0, tiled=True)
    out_grad = arrived.reshape(BLOCK, COMP)
    me = lax.axis_index("tower")
    slot = jnp.sum(jnp.where(feature_slot[0] == me, jnp.arange(CHIPS * CORES, dtype=jnp.int32), 0))
    place = jnp.stack([me & 1, me >> 1, me, slot]).astype(jnp.int32)
    inputs, down_mat, up_mat, comp_mat = pooled_in[0], w_down[0], w_up[0], w_comp[0]

    partner = lax.ppermute(inputs, "tower", SWAP)
    mine, *sent = call(
        pack_kernel,
        place,
        [inputs, partner, down_mat],
        [half_type(*TILE)] + [half_type(2, *TILE)] * NEAR + [half_type(*TILE)],
        "low_rank_and_columns",
        PACK_FLOPS,
        3_000_000,
    )
    received = [
        lax.ppermute(block, "tower", both_ways(step)) for step, block in enumerate(sent, 1)
    ]

    rows_out = rank_rows(out_grad, inputs, comp_mat, up_mat)
    rows_out, *received = lax.optimization_barrier((rows_out, *received))
    grads_own = lax.all_to_all(
        rows_out,
        "tower",
        split_axis=0,
        concat_axis=0,
        tiled=True,
        axis_index_groups=SAME_CORE,
    ).reshape(HALF, COMP + RANK)

    eight = half_type(CHIPS, 3, BLOCK, EMBED)
    keep, give = call(merge_kernel, place, [mine, *received], [eight, eight], "merge_rows")
    taken = lax.ppermute(give, "tower", SWAP)
    lengths = bag_lengths[0]
    counts, spread = call(
        counts_kernel,
        place,
        [jnp.transpose(bag_ids[0, 0]), lengths, 1.0 / lengths.astype(jnp.float32)],
        [half_type(CORES, TABLE_ROWS, HALF), full_type(CORES, HALF, EMBED)],
        "bag_counts",
    )
    low, x, crossed, scale, comp_two, down_one = call(
        saved_kernel,
        place,
        [keep, taken, down_mat, up_mat, cross_bias, comp_mat],
        [
            half_type(CORES, HALF, RANK),
            half_type(CORES, HALF, EMBED),
            half_type(CORES, HALF, EMBED),
            full_type(CORES, HALF, EMBED),
            half_type(2 * EMBED, COMP),
            half_type(EMBED, RANK),
        ],
        "saved_rows",
    )
    saved = (low, x, crossed, scale, counts, spread, comp_two, down_one)
    grads_own, *saved = lax.optimization_barrier((grads_own, *saved))
    grads_other = lax.ppermute(grads_own, "tower", SWAP)
    first = half(0, grads_own, saved)
    grad_down, grad_up, grad_bias, grad_comp, tables = half(1, grads_other, saved, first)
    return grad_down[None], grad_up[None], grad_bias, grad_comp[None], tables[None, None]


def solution(mesh):
    placed = (
        P(("tower", "hst"), None, None),
        P("hst", "tower", None),
        P("hst", None, None),
        P("hst", None, None),
        P("hst", None),
        P("hst", None, None),
        P("hst", None),
        P("hst", "tower", None, None),
        P("hst", "tower", None),
    )
    return jax.shard_map(
        on_device,
        mesh=mesh,
        in_specs=placed,
        out_specs=(
            P("hst", "tower", None),
            P("hst", None, "tower"),
            P("hst", "tower"),
            P("hst", "tower", None),
            P("hst", "tower", None, None),
        ),
        check_vma=False,
    )
```

```python
import jax
import jax.numpy as jnp
from jax import lax
from jax.experimental import pallas as pl
from jax.experimental.pallas import tpu as pltpu
from jax.sharding import PartitionSpec as P

EMBED = 128
COMP = 256
RANK = 256
TABLE_ROWS = 512
SLOTS = 8
CHIPS = 8
CORES = 2
BLOCK = 128
HALF = CHIPS * BLOCK

STEPS = 2
ROOM = 60 * 1024 * 1024
PACK_FLOPS = 270_000_000
RANK_FLOPS = 270_000_000
COUNTS_FLOPS = 32_000_000_000

NEAR = CHIPS // 2 - 1
SAME_CORE = [[chip * CORES + core for chip in range(CHIPS)] for core in range(CORES)]
SWAP = [(t, t ^ 1) for t in range(CHIPS * CORES)]


def both_ways(step):
    pairs = []
    for chip in range(CHIPS):
        pairs.append((chip * CORES, (chip + step) % CHIPS * CORES))
        pairs.append((chip * CORES + 1, (chip - step) % CHIPS * CORES + 1))
    return pairs


def contract_rows(left, right):
    return lax.dot_general(
        left, right, (((0,), (0,)), ((), ())), preferred_element_type=jnp.float32
    )


def contract_cols(left, right):
    return lax.dot_general(
        left, right, (((1,), (1,)), ((), ())), preferred_element_type=jnp.float32
    )


def product(left, right):
    return jnp.dot(left, right, preferred_element_type=jnp.float32)


def half_kernel(*refs):
    grads_ref, low_ref, x_ref, crossed_ref, scale_ref, counts_ref, spread_ref, comp_ref, down_ref = (
        refs[:9]
    )
    before, out_refs = refs[9:-5], refs[-5:]

    @pl.when(pl.program_id(0) == 0)
    def _():
        for index, ref in enumerate(out_refs):
            ref[...] = before[index][...] if before else jnp.zeros(ref.shape, ref.dtype)

    out_grad = grads_ref[:, :COMP]
    rank_grad = grads_ref[:, COMP:]
    x = x_ref[0]
    cross = contract_cols(out_grad, comp_ref[...])
    back = contract_cols(rank_grad, down_ref[...])
    input_grad = (cross[:, EMBED:] * scale_ref[0] + back).astype(jnp.bfloat16)
    scaled = input_grad.astype(jnp.float32) * spread_ref[0]
    high = scaled.astype(jnp.bfloat16)
    rest = (scaled - high.astype(jnp.float32)).astype(jnp.bfloat16)
    table = product(counts_ref[0], jnp.concatenate([high, rest], axis=1))
    scale_grad = (cross[:, :EMBED] * x.astype(jnp.float32)).astype(jnp.bfloat16)
    down_out, up_out, bias_out, comp_out, table_out = out_refs
    down_out[...] += contract_rows(x, rank_grad)
    up_out[...] += contract_rows(low_ref[0], scale_grad)
    bias_out[...] += jnp.sum(scale_grad.astype(jnp.float32), axis=0, keepdims=True)
    comp_out[...] += contract_rows(crossed_ref[0], out_grad)
    table_out[...] += table[:, :EMBED] + table[:, EMBED:]


def half(side, grads, saved, before=()):
    step = HALF // STEPS
    shapes = [(EMBED, RANK), (RANK, EMBED), (1, EMBED), (EMBED, COMP), (TABLE_ROWS, EMBED)]

    def rows(width):
        return pl.BlockSpec((1, step, width), lambda i: (side, i, 0))

    in_specs = [
        pl.BlockSpec((step, COMP + RANK), lambda i: (i, 0)),
        rows(RANK),
        rows(EMBED),
        rows(EMBED),
        rows(EMBED),
        pl.BlockSpec((1, TABLE_ROWS, step), lambda i: (side, 0, i)),
        rows(EMBED),
        fetched((2 * EMBED, COMP)),
        fetched((EMBED, RANK)),
    ] + [fetched(array.shape) for array in before]
    return pl.pallas_call(
        half_kernel,
        grid=(STEPS,),
        in_specs=in_specs,
        out_specs=[fetched(shape) for shape in shapes],
        out_shape=[full_type(*shape) for shape in shapes],
        compiler_params=pltpu.CompilerParams(vmem_limit_bytes=ROOM),
        cost_estimate=pl.CostEstimate(
            flops=1_500_000_000, bytes_accessed=6_000_000, transcendentals=0
        ),
        name="column_half_second" if before else "column_half_first",
    )(grads, *saved, *before)


def pack_kernel(
    x_ref, partner_ref, down_ref, self_ref, first_ref, second_ref, third_ref, far_ref
):
    _, core, chip = where_am_i()
    way = 1 - 2 * core
    sides = []
    for ref in (x_ref, partner_ref):
        low = product(ref[...], down_ref[...]).astype(jnp.bfloat16)
        sides.append((ref, low))

    def fill(step, side, target):
        ref, low = sides[side]
        base = lax.rem(chip + way * step + CHIPS, CHIPS) * CORES
        for part, slot in ((0, base + core), (3, base + 1 - core)):
            target[part] = ref[:, pl.ds(pl.multiple_of(slot * EMBED, EMBED), EMBED)]
        target[1] = low[:, :BLOCK]
        target[2] = low[:, BLOCK:]

    for step, near_ref in enumerate((first_ref, second_ref, third_ref), 1):
        for side in range(2):
            fill(step, side, near_ref.at[side])
    fill(CHIPS // 2, 0, far_ref)
    fill(0, 0, self_ref)


WHOLE = pl.BlockSpec(memory_space=pltpu.VMEM)
SCALARS = pl.BlockSpec(memory_space=pltpu.SMEM)


def fetched(shape):
    return pl.BlockSpec(shape, lambda i: (0,) * len(shape))


def where_am_i():
    me = lax.axis_index("tower")
    return me, me & 1, me >> 1


def call(kernel, operands, shapes, name, flops=1000, moved=1000, scalars=()):
    return pl.pallas_call(
        kernel,
        grid=(1,),
        in_specs=[SCALARS] * len(scalars) + [fetched(operand.shape) for operand in operands],
        out_specs=[fetched(shape.shape) for shape in shapes],
        out_shape=shapes,
        compiler_params=pltpu.CompilerParams(vmem_limit_bytes=ROOM),
        cost_estimate=pl.CostEstimate(flops=flops, bytes_accessed=moved, transcendentals=0),
        name=name,
    )(*scalars, *operands)


def half_type(*shape):
    return jax.ShapeDtypeStruct(shape, jnp.bfloat16)


def full_type(*shape):
    return jax.ShapeDtypeStruct(shape, jnp.float32)


TILE = (4, BLOCK, EMBED)


def merge_kernel(
    self_ref, first_ref, second_ref, third_ref, far_ref, keep_ref, give_ref
):
    blocks = [self_ref]
    for ref in (first_ref, second_ref, third_ref):
        blocks += [ref.at[0], ref.at[1]]
    blocks.append(far_ref)
    for index, block in enumerate(blocks):
        keep_ref[index] = block[0:3]
        give_ref[index] = block[1:4]


def counts_kernel(ids_ref, lengths_ref, inverse_ref, counts_ref, spread_ref):
    _, mine, _ = where_am_i()
    tile = 64

    @pl.loop(0, CHIPS * CORES)
    def _(block):
        side = jnp.where(lax.rem(block, CORES) == mine, 0, 1)
        bags = pl.ds(pl.multiple_of(block * BLOCK, BLOCK), BLOCK)
        to = pl.ds(pl.multiple_of(lax.div(block, CORES) * BLOCK, BLOCK), BLOCK)
        lengths = lengths_ref[:, bags]
        live = [
            jnp.where(lengths > slot, ids_ref[slot : slot + 1, bags], -1) for slot in range(SLOTS)
        ]
        for start in range(0, TABLE_ROWS, tile):
            row_values = start + lax.broadcasted_iota(jnp.int32, (tile, BLOCK), 0)
            total = jnp.zeros((tile, BLOCK), jnp.float32)
            for slot in range(SLOTS):
                total = total + jnp.where(live[slot] == row_values, 1.0, 0.0)
            counts_ref[side, start : start + tile, to] = total.astype(jnp.bfloat16)
        spread_ref[side, to, :] = jnp.broadcast_to(inverse_ref[:, bags], (BLOCK, BLOCK)).T


def saved_kernel(
    slots_ref,
    keep_ref,
    taken_ref,
    down_ref,
    up_ref,
    bias_ref,
    comp_ref,
    low_ref,
    x_ref,
    crossed_ref,
    scale_ref,
    comp_out,
    down_out,
):
    me, mine, chip = where_am_i()
    slot = jnp.int32(0)
    for index in range(CHIPS * CORES):
        slot = jnp.where(slots_ref[0, index] == me, index, slot)
    own = pl.ds(pl.multiple_of(me * EMBED, EMBED), EMBED)
    served = pl.ds(pl.multiple_of(slot * EMBED, EMBED), EMBED)
    comp_out[:EMBED, :] = comp_ref[own, :]
    comp_out[EMBED:, :] = comp_ref[served, :]
    down_out[...] = down_ref[served, :]
    ups = jnp.concatenate([up_ref[:, own], up_ref[:, served]], axis=1)
    bias = jnp.concatenate([bias_ref[:, own], bias_ref[:, served]], axis=1)
    for side in range(CORES):
        core = mine if side == 0 else 1 - mine

        @pl.loop(0, CHIPS)
        def _(k):
            rows = pl.ds(pl.multiple_of(k * BLOCK, BLOCK), BLOCK)
            way = lax.rem((chip - k) * (1 - 2 * mine) + CHIPS, CHIPS)
            given = (way > CHIPS // 2) | ((lax.rem(way, CHIPS // 2) == 0) & (core != mine))
            near = jnp.where(way > CHIPS // 2, CHIPS - way, way)
            holder = jnp.where(given, 1 - mine, mine)
            inner = 2 * near - 1 + jnp.where(core == holder, 0, 1)
            at = jnp.where(near == 0, 0, jnp.where(near == CHIPS // 2, CHIPS - 1, inner))

            @pl.when(given)
            def _():
                x_ref[side, rows, :] = taken_ref[at, 2]
                low_ref[side, rows, :BLOCK] = taken_ref[at, 0]
                low_ref[side, rows, BLOCK:] = taken_ref[at, 1]

            @pl.when(jnp.logical_not(given))
            def _():
                x_ref[side, rows, :] = keep_ref[at, 0]
                low_ref[side, rows, :BLOCK] = keep_ref[at, 1]
                low_ref[side, rows, BLOCK:] = keep_ref[at, 2]

        scale = product(low_ref[side], ups) + bias
        wide = x_ref[side].astype(jnp.float32)
        crossed_ref[side] = (wide * scale[:, :EMBED] + wide).astype(jnp.bfloat16)
        scale_ref[side] = scale[:, EMBED:] + 1.0


def rank_kernel(grad_ref, x_ref, comp_ref, up_ref, out_ref):
    out_grad = grad_ref[...]
    total = jnp.zeros((BLOCK, RANK), jnp.float32)
    width = 512
    for start in range(0, x_ref.shape[1], width):
        columns = pl.ds(start, width)
        cross = contract_cols(out_grad, comp_ref[columns, :])
        scale_grad = (cross * x_ref[:, columns].astype(jnp.float32)).astype(jnp.bfloat16)
        total += contract_cols(scale_grad, up_ref[:, columns])
    rank_grad = total.astype(jnp.bfloat16)
    for chip in range(CHIPS):
        out_ref[chip, :, :COMP] = out_grad
        out_ref[chip, :, COMP:] = rank_grad


def rank_rows(out_grad, inputs, comp_mat, up_mat):
    return pl.pallas_call(
        rank_kernel,
        in_specs=[WHOLE] * 4,
        out_specs=WHOLE,
        out_shape=jax.ShapeDtypeStruct((CHIPS, BLOCK, COMP + RANK), jnp.bfloat16),
        compiler_params=pltpu.CompilerParams(vmem_limit_bytes=16 * 1024 * 1024),
        cost_estimate=pl.CostEstimate(
            flops=RANK_FLOPS, bytes_accessed=3_600_000, transcendentals=0
        ),
        name="rank_grad_rows",
    )(out_grad, inputs, comp_mat, up_mat)


def on_device(
    top_grad, pooled_in, w_down, w_up, cross_bias, w_comp, feature_slot, bag_ids, bag_lengths
):
    arrived = lax.all_to_all(top_grad, "hst", split_axis=1, concat_axis=0, tiled=True)
    out_grad = arrived.reshape(BLOCK, COMP)
    inputs, down_mat, up_mat, comp_mat = pooled_in[0], w_down[0], w_up[0], w_comp[0]

    partner = lax.ppermute(inputs, "tower", SWAP)
    mine, *sent = call(
        pack_kernel,
        [inputs, partner, down_mat],
        [half_type(*TILE)] + [half_type(2, *TILE)] * NEAR + [half_type(*TILE)],
        "low_rank_and_columns",
        PACK_FLOPS,
        3_000_000,
    )
    received = [
        lax.ppermute(block, "tower", both_ways(step)) for step, block in enumerate(sent, 1)
    ]

    rows_out = rank_rows(out_grad, inputs, comp_mat, up_mat)
    grads_own = lax.all_to_all(
        rows_out,
        "tower",
        split_axis=0,
        concat_axis=0,
        tiled=True,
        axis_index_groups=SAME_CORE,
    ).reshape(HALF, COMP + RANK)

    eight = half_type(CHIPS, 3, BLOCK, EMBED)
    keep, give = call(merge_kernel, [mine, *received], [eight, eight], "merge_rows")
    taken = lax.ppermute(give, "tower", SWAP)
    lengths = bag_lengths[0]
    counts, spread = call(
        counts_kernel,
        [jnp.transpose(bag_ids[0, 0]), lengths, 1.0 / lengths.astype(jnp.float32)],
        [half_type(CORES, TABLE_ROWS, HALF), full_type(CORES, HALF, EMBED)],
        "bag_counts",
        COUNTS_FLOPS,
    )
    low, x, crossed, scale, comp_two, down_one = call(
        saved_kernel,
        [keep, taken, down_mat, up_mat, cross_bias, comp_mat],
        [
            half_type(CORES, HALF, RANK),
            half_type(CORES, HALF, EMBED),
            half_type(CORES, HALF, EMBED),
            full_type(CORES, HALF, EMBED),
            half_type(2 * EMBED, COMP),
            half_type(EMBED, RANK),
        ],
        "saved_rows",
        scalars=[feature_slot],
    )
    saved = (low, x, crossed, scale, counts, spread, comp_two, down_one)
    grads_own, *saved = lax.optimization_barrier((grads_own, *saved))
    grads_other = lax.ppermute(grads_own, "tower", SWAP)
    first = half(0, grads_own, saved)
    grad_down, grad_up, grad_bias, grad_comp, tables = half(1, grads_other, saved, first)
    return grad_down[None], grad_up[None], grad_bias, grad_comp[None], tables[None, None]


def solution(mesh):
    placed = (
        P(("tower", "hst"), None, None),
        P("hst", "tower", None),
        P("hst", None, None),
        P("hst", None, None),
        P("hst", None),
        P("hst", None, None),
        P("hst", None),
        P("hst", "tower", None, None),
        P("hst", "tower", None),
    )
    return jax.shard_map(
        on_device,
        mesh=mesh,
        in_specs=placed,
        out_specs=(
            P("hst", "tower", None),
            P("hst", None, "tower"),
            P("hst", "tower"),
            P("hst", "tower", None),
            P("hst", "tower", None, None),
        ),
        check_vma=False,
    )
```

```python
import jax
import jax.numpy as jnp
from jax import lax
from jax.experimental import pallas as pl
from jax.experimental.pallas import tpu as pltpu
from jax.sharding import PartitionSpec as P

EMBED = 128
COMP = 256
RANK = 256
TABLE_ROWS = 512
SLOTS = 8
CHIPS = 8
CORES = 2
BLOCK = 128
HALF = CHIPS * BLOCK

STEPS = 2
ROOM = 60 * 1024 * 1024
PACK_FLOPS = 270_000_000
RANK_FLOPS = 270_000_000
MERGE_FLOPS = 16_000_000_000
COUNTS_FLOPS = 6_000_000_000

NEAR = CHIPS // 2 - 1
SAME_CORE = [[chip * CORES + core for chip in range(CHIPS)] for core in range(CORES)]
SWAP = [(t, t ^ 1) for t in range(CHIPS * CORES)]


def both_ways(step):
    pairs = []
    for chip in range(CHIPS):
        pairs.append((chip * CORES, (chip + step) % CHIPS * CORES))
        pairs.append((chip * CORES + 1, (chip - step) % CHIPS * CORES + 1))
    return pairs


def contract_rows(left, right):
    return lax.dot_general(
        left, right, (((0,), (0,)), ((), ())), preferred_element_type=jnp.float32
    )


def contract_cols(left, right):
    return lax.dot_general(
        left, right, (((1,), (1,)), ((), ())), preferred_element_type=jnp.float32
    )


def product(left, right):
    return jnp.dot(left, right, preferred_element_type=jnp.float32)


def half_kernel(*refs):
    grads_ref, low_ref, x_ref, crossed_ref, scale_ref, counts_ref, spread_ref, comp_ref, down_ref = (
        refs[:9]
    )
    before, out_refs, up_sum = refs[9:-6], refs[-6:-1], refs[-1]
    sums = list(out_refs)
    sums[1] = up_sum

    @pl.when(pl.program_id(0) == 0)
    def _():
        for index, ref in enumerate(sums):
            ref[...] = before[index][...] if before else jnp.zeros(ref.shape, ref.dtype)

    out_grad = grads_ref[:, :COMP]
    rank_grad = grads_ref[:, COMP:]
    x = x_ref[0]
    cross = contract_cols(out_grad, comp_ref[...])
    back = contract_cols(rank_grad, down_ref[...])
    input_grad = (cross[:, EMBED:] * scale_ref[0] + back).astype(jnp.bfloat16)
    scaled = input_grad.astype(jnp.float32) * spread_ref[0]
    high = scaled.astype(jnp.bfloat16)
    rest = (scaled - high.astype(jnp.float32)).astype(jnp.bfloat16)
    table = product(counts_ref[0], jnp.concatenate([high, rest], axis=1))
    scale_grad = (cross[:, :EMBED] * x.astype(jnp.float32)).astype(jnp.bfloat16)
    down_out, up_out, bias_out, comp_out, table_out = out_refs
    up_sum[...] += contract_rows(scale_grad, low_ref[0])
    down_out[...] += contract_rows(x, rank_grad)
    bias_out[...] += jnp.sum(scale_grad.astype(jnp.float32), axis=0, keepdims=True)
    comp_out[...] += contract_rows(crossed_ref[0], out_grad)
    table_out[...] += table[:, :EMBED] + table[:, EMBED:]

    @pl.when(pl.program_id(0) == pl.num_programs(0) - 1)
    def _():
        up_out[...] = up_sum[...].T if before else up_sum[...]


def half(side, grads, saved, before=()):
    step = HALF // STEPS
    shapes = [(EMBED, RANK), (EMBED, RANK), (1, EMBED), (EMBED, COMP), (TABLE_ROWS, EMBED)]
    if before:
        shapes[1] = (RANK, EMBED)

    def rows(width):
        return pl.BlockSpec((1, step, width), lambda i: (side, i, 0))

    in_specs = [
        pl.BlockSpec((step, COMP + RANK), lambda i: (i, 0)),
        rows(RANK),
        rows(EMBED),
        rows(EMBED),
        rows(EMBED),
        pl.BlockSpec((1, TABLE_ROWS, step), lambda i: (side, 0, i)),
        rows(EMBED),
        fetched((2 * EMBED, COMP)),
        fetched((EMBED, RANK)),
    ] + [fetched(array.shape) for array in before]
    return pl.pallas_call(
        half_kernel,
        grid=(STEPS,),
        in_specs=in_specs,
        out_specs=[fetched(shape) for shape in shapes],
        out_shape=[full_type(*shape) for shape in shapes],
        scratch_shapes=[pltpu.VMEM((EMBED, RANK), jnp.float32)],
        compiler_params=pltpu.CompilerParams(vmem_limit_bytes=ROOM),
        cost_estimate=pl.CostEstimate(
            flops=1_500_000_000, bytes_accessed=6_000_000, transcendentals=0
        ),
        name="column_half_second" if before else "column_half_first",
    )(grads, *saved, *before)


def pack_kernel(
    x_ref, partner_ref, down_ref, self_ref, first_ref, second_ref, third_ref, far_ref
):
    _, core, chip = where_am_i()
    way = 1 - 2 * core
    sides = []
    for ref in (x_ref, partner_ref):
        low = product(ref[...], down_ref[...]).astype(jnp.bfloat16)
        sides.append((ref, low))

    def fill(step, side, target):
        ref, low = sides[side]
        base = lax.rem(chip + way * step + CHIPS, CHIPS) * CORES
        for part, slot in ((0, base + core), (3, base + 1 - core)):
            target[part] = ref[:, pl.ds(pl.multiple_of(slot * EMBED, EMBED), EMBED)]
        target[1] = low[:, :BLOCK]
        target[2] = low[:, BLOCK:]

    for step, near_ref in enumerate((first_ref, second_ref, third_ref), 1):
        for side in range(2):
            fill(step, side, near_ref.at[side])
    fill(CHIPS // 2, 0, far_ref)
    fill(0, 0, self_ref)


WHOLE = pl.BlockSpec(memory_space=pltpu.VMEM)
SCALARS = pl.BlockSpec(memory_space=pltpu.SMEM)


def fetched(shape):
    return pl.BlockSpec(shape, lambda i: (0,) * len(shape))


def where_am_i():
    me = lax.axis_index("tower")
    return me, me & 1, me >> 1


def call(kernel, operands, shapes, name, flops=1000, moved=1000, scalars=()):
    return pl.pallas_call(
        kernel,
        grid=(1,),
        in_specs=[SCALARS] * len(scalars) + [fetched(operand.shape) for operand in operands],
        out_specs=[fetched(shape.shape) for shape in shapes],
        out_shape=shapes,
        compiler_params=pltpu.CompilerParams(vmem_limit_bytes=ROOM),
        cost_estimate=pl.CostEstimate(flops=flops, bytes_accessed=moved, transcendentals=0),
        name=name,
    )(*scalars, *operands)


def half_type(*shape):
    return jax.ShapeDtypeStruct(shape, jnp.bfloat16)


def full_type(*shape):
    return jax.ShapeDtypeStruct(shape, jnp.float32)


TILE = (4, BLOCK, EMBED)


def in_order(self_ref, first_ref, second_ref, third_ref, far_ref):
    blocks = [self_ref]
    for ref in (first_ref, second_ref, third_ref):
        blocks += [ref.at[0], ref.at[1]]
    return blocks + [far_ref]


def merge_kernel(*refs):
    give_ref = refs[-1]
    for index, block in enumerate(in_order(*refs[:-1])):
        give_ref[index] = block[1:4]


def counts_kernel(ids_ref, lengths_ref, inverse_ref, counts_ref, spread_ref):
    _, mine, _ = where_am_i()
    tile = 64
    middle = TABLE_ROWS // 2
    narrow = jnp.bfloat16

    @pl.loop(0, CHIPS * CORES)
    def _(block):
        side = jnp.where(lax.rem(block, CORES) == mine, 0, 1)
        bags = pl.ds(pl.multiple_of(block * BLOCK, BLOCK), BLOCK)
        to = pl.ds(pl.multiple_of(lax.div(block, CORES) * BLOCK, BLOCK), BLOCK)
        lengths = lengths_ref[:, bags]
        live = [
            jnp.broadcast_to(
                jnp.where(lengths > slot, ids_ref[slot : slot + 1, bags] - middle, TABLE_ROWS)
                .astype(jnp.float32)
                .astype(narrow),
                (tile, BLOCK),
            )
            for slot in range(SLOTS)
        ]
        offsets = lax.broadcasted_iota(jnp.int32, (tile, BLOCK), 0).astype(jnp.float32)
        for start in range(0, TABLE_ROWS, tile):
            row_values = (offsets + float(start - middle)).astype(narrow)
            total = jnp.zeros((tile, BLOCK), narrow)
            for slot in range(SLOTS):
                total = total + jnp.where(live[slot] == row_values, narrow(1), narrow(0))
            counts_ref[side, start : start + tile, to] = total
        spread_ref[side, to, :] = jnp.broadcast_to(inverse_ref[:, bags], (BLOCK, BLOCK)).T


def saved_kernel(
    slots_ref,
    self_ref,
    first_ref,
    second_ref,
    third_ref,
    far_ref,
    taken_ref,
    down_ref,
    up_ref,
    bias_ref,
    comp_ref,
    low_ref,
    x_ref,
    crossed_ref,
    scale_ref,
    comp_out,
    down_out,
):
    me, mine, chip = where_am_i()
    slot = jnp.int32(0)
    for index in range(CHIPS * CORES):
        slot = jnp.where(slots_ref[0, index] == me, index, slot)
    own = pl.ds(pl.multiple_of(me * EMBED, EMBED), EMBED)
    served = pl.ds(pl.multiple_of(slot * EMBED, EMBED), EMBED)
    comp_out[:EMBED, :] = comp_ref[own, :]
    comp_out[EMBED:, :] = comp_ref[served, :]
    down_out[...] = down_ref[served, :]
    ups = jnp.concatenate([up_ref[:, own], up_ref[:, served]], axis=1)
    bias = jnp.concatenate([bias_ref[:, own], bias_ref[:, served]], axis=1)
    kept = in_order(self_ref, first_ref, second_ref, third_ref, far_ref)
    for given in range(2):
        holder = 1 - mine if given else mine
        for index in range(CHIPS):
            near = (index + 1) // 2
            opposite = index % 2 == 0 and index > 0
            side = given ^ opposite
            k = lax.rem(chip + (2 * holder - 1) * near + CHIPS, CHIPS)
            rows = pl.ds(pl.multiple_of(k * BLOCK, BLOCK), BLOCK)
            if given:
                low_low, low_high, x = (taken_ref[index, part] for part in range(3))
            else:
                x, low_low, low_high = (kept[index][part] for part in range(3))
            x_ref[side, rows, :] = x
            low_ref[side, rows, :BLOCK] = low_low
            low_ref[side, rows, BLOCK:] = low_high
    for side in range(CORES):
        scale = product(low_ref[side], ups) + bias
        wide = x_ref[side].astype(jnp.float32)
        crossed_ref[side] = (wide * scale[:, :EMBED] + wide).astype(jnp.bfloat16)
        scale_ref[side] = scale[:, EMBED:] + 1.0


def rank_kernel(grad_ref, x_ref, comp_ref, up_ref, out_ref):
    out_grad = grad_ref[...]
    total = jnp.zeros((BLOCK, RANK), jnp.float32)
    width = 512
    for start in range(0, x_ref.shape[1], width):
        columns = pl.ds(start, width)
        cross = contract_cols(out_grad, comp_ref[columns, :])
        scale_grad = (cross * x_ref[:, columns].astype(jnp.float32)).astype(jnp.bfloat16)
        total += contract_cols(scale_grad, up_ref[:, columns])
    rank_grad = total.astype(jnp.bfloat16)
    for chip in range(CHIPS):
        out_ref[chip, :, :COMP] = out_grad
        out_ref[chip, :, COMP:] = rank_grad


def rank_rows(out_grad, inputs, comp_mat, up_mat):
    return pl.pallas_call(
        rank_kernel,
        in_specs=[WHOLE] * 4,
        out_specs=WHOLE,
        out_shape=jax.ShapeDtypeStruct((CHIPS, BLOCK, COMP + RANK), jnp.bfloat16),
        compiler_params=pltpu.CompilerParams(vmem_limit_bytes=16 * 1024 * 1024),
        cost_estimate=pl.CostEstimate(
            flops=RANK_FLOPS, bytes_accessed=3_600_000, transcendentals=0
        ),
        name="rank_grad_rows",
    )(out_grad, inputs, comp_mat, up_mat)


def on_device(
    top_grad, pooled_in, w_down, w_up, cross_bias, w_comp, feature_slot, bag_ids, bag_lengths
):
    arrived = lax.all_to_all(top_grad, "hst", split_axis=1, concat_axis=0, tiled=True)
    out_grad = arrived.reshape(BLOCK, COMP)
    inputs, down_mat, up_mat, comp_mat = pooled_in[0], w_down[0], w_up[0], w_comp[0]

    partner = lax.ppermute(inputs, "tower", SWAP)
    mine, *sent = call(
        pack_kernel,
        [inputs, partner, down_mat],
        [half_type(*TILE)] + [half_type(2, *TILE)] * NEAR + [half_type(*TILE)],
        "low_rank_and_columns",
        PACK_FLOPS,
        3_000_000,
    )
    received = [
        lax.ppermute(block, "tower", both_ways(step)) for step, block in enumerate(sent, 1)
    ]

    rows_out = rank_rows(out_grad, inputs, comp_mat, up_mat)
    grads_own = lax.all_to_all(
        rows_out,
        "tower",
        split_axis=0,
        concat_axis=0,
        tiled=True,
        axis_index_groups=SAME_CORE,
    ).reshape(HALF, COMP + RANK)

    lengths = bag_lengths[0]
    counts, spread = call(
        counts_kernel,
        [jnp.transpose(bag_ids[0, 0]), lengths, 1.0 / lengths.astype(jnp.float32)],
        [half_type(CORES, TABLE_ROWS, HALF), full_type(CORES, HALF, EMBED)],
        "bag_counts",
        COUNTS_FLOPS,
    )
    counts, *received = lax.optimization_barrier((counts, *received))
    eight = half_type(CHIPS, 3, BLOCK, EMBED)
    (give,) = call(merge_kernel, [mine, *received], [eight], "merge_rows", MERGE_FLOPS)
    taken = lax.ppermute(give, "tower", SWAP)
    low, x, crossed, scale, comp_two, down_one = call(
        saved_kernel,
        [mine, *received, taken, down_mat, up_mat, cross_bias, comp_mat],
        [
            half_type(CORES, HALF, RANK),
            half_type(CORES, HALF, EMBED),
            half_type(CORES, HALF, EMBED),
            full_type(CORES, HALF, EMBED),
            half_type(2 * EMBED, COMP),
            half_type(EMBED, RANK),
        ],
        "saved_rows",
        scalars=[feature_slot],
    )
    saved = (low, x, crossed, scale, counts, spread, comp_two, down_one)
    grads_own, *saved = lax.optimization_barrier((grads_own, *saved))
    grads_other = lax.ppermute(grads_own, "tower", SWAP)
    first = half(0, grads_own, saved)
    grad_down, grad_up, grad_bias, grad_comp, tables = half(1, grads_other, saved, first)
    return grad_down[None], grad_up[None], grad_bias, grad_comp[None], tables[None, None]


def solution(mesh):
    placed = (
        P(("tower", "hst"), None, None),
        P("hst", "tower", None),
        P("hst", None, None),
        P("hst", None, None),
        P("hst", None),
        P("hst", None, None),
        P("hst", None),
        P("hst", "tower", None, None),
        P("hst", "tower", None),
    )
    return jax.shard_map(
        on_device,
        mesh=mesh,
        in_specs=placed,
        out_specs=(
            P("hst", "tower", None),
            P("hst", None, "tower"),
            P("hst", "tower"),
            P("hst", "tower", None),
            P("hst", "tower", None, None),
        ),
        check_vma=False,
    )
```

```python
import jax
import jax.numpy as jnp
from jax import lax
from jax.experimental import pallas as pl
from jax.experimental.pallas import tpu as pltpu
from jax.sharding import PartitionSpec as P

EMBED = 128
COMP = 256
RANK = 256
TABLE_ROWS = 512
SLOTS = 8
CHIPS = 8
CORES = 2
BLOCK = 128
HALF = CHIPS * BLOCK

STEPS = 2
ROOM = 60 * 1024 * 1024
HALF_ROOM = 60 * 1024 * 1024
PACK_FLOPS = 270_000_000
RANK_FLOPS = 270_000_000
MERGE_FLOPS = 16_000_000_000
COUNTS_FLOPS = 500_000_000

NEAR = CHIPS // 2 - 1
SAME_CORE = [[chip * CORES + core for chip in range(CHIPS)] for core in range(CORES)]
SWAP = [(t, t ^ 1) for t in range(CHIPS * CORES)]


def both_ways(step):
    pairs = []
    for chip in range(CHIPS):
        pairs.append((chip * CORES, (chip + step) % CHIPS * CORES))
        pairs.append((chip * CORES + 1, (chip - step) % CHIPS * CORES + 1))
    return pairs


def contract_rows(left, right):
    return lax.dot_general(
        left, right, (((0,), (0,)), ((), ())), preferred_element_type=jnp.float32
    )


def contract_cols(left, right):
    return lax.dot_general(
        left, right, (((1,), (1,)), ((), ())), preferred_element_type=jnp.float32
    )


def product(left, right):
    return jnp.dot(left, right, preferred_element_type=jnp.float32)


def half_kernel(*refs):
    grads_ref, low_ref, x_ref, crossed_ref, scale_ref, counts_ref, spread_ref, comp_ref, down_ref = (
        refs[:9]
    )
    before, out_refs, up_sum = refs[9:-6], refs[-6:-1], refs[-1]
    sums = list(out_refs)
    sums[1] = up_sum

    @pl.when(pl.program_id(0) == 0)
    def _():
        for index, ref in enumerate(sums):
            ref[...] = before[index][...] if before else jnp.zeros(ref.shape, ref.dtype)

    out_grad = grads_ref[:, :COMP]
    rank_grad = grads_ref[:, COMP:]
    x = x_ref[0]
    cross = contract_cols(out_grad, comp_ref[...])
    back = contract_cols(rank_grad, down_ref[...])
    input_grad = (cross[:, EMBED:] * scale_ref[0] + back).astype(jnp.bfloat16)
    scaled = input_grad.astype(jnp.float32) * spread_ref[0]
    high = scaled.astype(jnp.bfloat16)
    rest = (scaled - high.astype(jnp.float32)).astype(jnp.bfloat16)
    table = product(counts_ref[0], jnp.concatenate([high, rest], axis=1))
    scale_grad = (cross[:, :EMBED] * x.astype(jnp.float32)).astype(jnp.bfloat16)
    down_out, up_out, bias_out, comp_out, table_out = out_refs
    up_sum[...] += contract_rows(scale_grad, low_ref[0])
    down_out[...] += contract_rows(x, rank_grad)
    bias_out[...] += jnp.sum(scale_grad.astype(jnp.float32), axis=0, keepdims=True)
    comp_out[...] += contract_rows(crossed_ref[0], out_grad)
    table_out[...] += table[:, :EMBED] + table[:, EMBED:]

    @pl.when(pl.program_id(0) == pl.num_programs(0) - 1)
    def _():
        up_out[...] = up_sum[...].T if before else up_sum[...]


def half(side, grads, saved, before=()):
    step = HALF // STEPS
    shapes = [(EMBED, RANK), (EMBED, RANK), (1, EMBED), (EMBED, COMP), (TABLE_ROWS, EMBED)]
    if before:
        shapes[1] = (RANK, EMBED)

    def rows(width):
        return pl.BlockSpec((1, step, width), lambda i: (side, i, 0))

    in_specs = [
        pl.BlockSpec((step, COMP + RANK), lambda i: (i, 0)),
        rows(RANK),
        rows(EMBED),
        rows(EMBED),
        rows(EMBED),
        pl.BlockSpec((1, TABLE_ROWS, step), lambda i: (side, 0, i)),
        rows(EMBED),
        fetched((2 * EMBED, COMP)),
        fetched((EMBED, RANK)),
    ] + [fetched(array.shape) for array in before]
    return pl.pallas_call(
        half_kernel,
        grid=(STEPS,),
        in_specs=in_specs,
        out_specs=[fetched(shape) for shape in shapes],
        out_shape=[full_type(*shape) for shape in shapes],
        scratch_shapes=[pltpu.VMEM((EMBED, RANK), jnp.float32)],
        compiler_params=pltpu.CompilerParams(vmem_limit_bytes=HALF_ROOM),
        cost_estimate=pl.CostEstimate(
            flops=1_500_000_000, bytes_accessed=6_000_000, transcendentals=0
        ),
        name="column_half_second" if before else "column_half_first",
    )(grads, *saved, *before)


def pack_kernel(
    x_ref, partner_ref, down_ref, self_ref, first_ref, second_ref, third_ref, far_ref
):
    _, core, chip = where_am_i()
    way = 1 - 2 * core
    sides = []
    for ref in (x_ref, partner_ref):
        low = product(ref[...], down_ref[...]).astype(jnp.bfloat16)
        sides.append((ref, low))

    def fill(step, side, target):
        ref, low = sides[side]
        base = lax.rem(chip + way * step + CHIPS, CHIPS) * CORES
        for part, slot in ((0, base + core), (3, base + 1 - core)):
            target[part] = ref[:, pl.ds(pl.multiple_of(slot * EMBED, EMBED), EMBED)]
        target[1] = low[:, :BLOCK]
        target[2] = low[:, BLOCK:]

    for step, near_ref in enumerate((first_ref, second_ref, third_ref), 1):
        for side in range(2):
            fill(step, side, near_ref.at[side])
    fill(CHIPS // 2, 0, far_ref)
    fill(0, 0, self_ref)


WHOLE = pl.BlockSpec(memory_space=pltpu.VMEM)
SCALARS = pl.BlockSpec(memory_space=pltpu.SMEM)


def fetched(shape):
    return pl.BlockSpec(shape, lambda i: (0,) * len(shape))


def where_am_i():
    me = lax.axis_index("tower")
    return me, me & 1, me >> 1


def call(kernel, operands, shapes, name, flops=1000, moved=1000, scalars=()):
    return pl.pallas_call(
        kernel,
        grid=(1,),
        in_specs=[SCALARS] * len(scalars) + [fetched(operand.shape) for operand in operands],
        out_specs=[fetched(shape.shape) for shape in shapes],
        out_shape=shapes,
        compiler_params=pltpu.CompilerParams(vmem_limit_bytes=ROOM),
        cost_estimate=pl.CostEstimate(flops=flops, bytes_accessed=moved, transcendentals=0),
        name=name,
    )(*scalars, *operands)


def half_type(*shape):
    return jax.ShapeDtypeStruct(shape, jnp.bfloat16)


def full_type(*shape):
    return jax.ShapeDtypeStruct(shape, jnp.float32)


TILE = (4, BLOCK, EMBED)


def in_order(self_ref, first_ref, second_ref, third_ref, far_ref):
    blocks = [self_ref]
    for ref in (first_ref, second_ref, third_ref):
        blocks += [ref.at[0], ref.at[1]]
    return blocks + [far_ref]


def merge_kernel(*refs):
    give_ref = refs[-1]
    for index, block in enumerate(in_order(*refs[:-1])):
        give_ref[index] = block[1:4]


def counts_kernel(ids_ref, lengths_ref, counts_ref, spread_ref):
    _, mine, _ = where_am_i()
    tile = 64
    middle = TABLE_ROWS // 2
    narrow = jnp.bfloat16

    @pl.loop(0, CHIPS * CORES)
    def _(block):
        side = jnp.where(lax.rem(block, CORES) == mine, 0, 1)
        bags = pl.ds(pl.multiple_of(block * BLOCK, BLOCK), BLOCK)
        to = pl.ds(pl.multiple_of(lax.div(block, CORES) * BLOCK, BLOCK), BLOCK)
        lengths = lengths_ref[:, bags]
        live = [
            jnp.broadcast_to(
                jnp.where(lengths > slot, ids_ref[slot : slot + 1, bags] - middle, TABLE_ROWS)
                .astype(jnp.float32)
                .astype(narrow),
                (tile, BLOCK),
            )
            for slot in range(SLOTS)
        ]
        offsets = lax.broadcasted_iota(jnp.int32, (tile, BLOCK), 0).astype(jnp.float32)
        for start in range(0, TABLE_ROWS, tile):
            row_values = (offsets + float(start - middle)).astype(narrow)
            total = jnp.zeros((tile, BLOCK), narrow)
            for slot in range(SLOTS):
                total = total + jnp.where(live[slot] == row_values, narrow(1), narrow(0))
            counts_ref[side, start : start + tile, to] = total
        spread_ref[side, to, :] = jnp.broadcast_to(
            1.0 / lengths.astype(jnp.float32), (BLOCK, BLOCK)
        ).T


def saved_kernel(
    slots_ref,
    self_ref,
    first_ref,
    second_ref,
    third_ref,
    far_ref,
    taken_ref,
    down_ref,
    up_ref,
    bias_ref,
    comp_ref,
    low_ref,
    x_ref,
    crossed_ref,
    scale_ref,
    comp_out,
    down_out,
):
    me, mine, chip = where_am_i()
    slot = jnp.int32(0)
    for index in range(CHIPS * CORES):
        slot = jnp.where(slots_ref[0, index] == me, index, slot)
    own = pl.ds(pl.multiple_of(me * EMBED, EMBED), EMBED)
    served = pl.ds(pl.multiple_of(slot * EMBED, EMBED), EMBED)
    comp_out[:EMBED, :] = comp_ref[own, :]
    comp_out[EMBED:, :] = comp_ref[served, :]
    down_out[...] = down_ref[served, :]
    ups = jnp.concatenate([up_ref[:, own], up_ref[:, served]], axis=1)
    bias = jnp.concatenate([bias_ref[:, own], bias_ref[:, served]], axis=1)
    kept = in_order(self_ref, first_ref, second_ref, third_ref, far_ref)
    for given in range(2):
        holder = 1 - mine if given else mine
        for index in range(CHIPS):
            near = (index + 1) // 2
            opposite = index % 2 == 0 and index > 0
            side = given ^ opposite
            k = lax.rem(chip + (2 * holder - 1) * near + CHIPS, CHIPS)
            rows = pl.ds(pl.multiple_of(k * BLOCK, BLOCK), BLOCK)
            if given:
                low_low, low_high, x = (taken_ref[index, part] for part in range(3))
            else:
                x, low_low, low_high = (kept[index][part] for part in range(3))
            x_ref[side, rows, :] = x
            low_ref[side, rows, :BLOCK] = low_low
            low_ref[side, rows, BLOCK:] = low_high
    for side in range(CORES):
        scale = product(low_ref[side], ups) + bias
        wide = x_ref[side].astype(jnp.float32)
        crossed_ref[side] = (wide * scale[:, :EMBED] + wide).astype(jnp.bfloat16)
        scale_ref[side] = scale[:, EMBED:] + 1.0


def rank_kernel(grad_ref, x_ref, comp_ref, up_ref, out_ref):
    out_grad = grad_ref[...]
    total = jnp.zeros((BLOCK, RANK), jnp.float32)
    width = 512
    for start in range(0, x_ref.shape[1], width):
        columns = pl.ds(start, width)
        cross = contract_cols(out_grad, comp_ref[columns, :])
        scale_grad = (cross * x_ref[:, columns].astype(jnp.float32)).astype(jnp.bfloat16)
        total += contract_cols(scale_grad, up_ref[:, columns])
    rank_grad = total.astype(jnp.bfloat16)
    for chip in range(CHIPS):
        out_ref[chip, :, :COMP] = out_grad
        out_ref[chip, :, COMP:] = rank_grad


def rank_rows(out_grad, inputs, comp_mat, up_mat):
    return pl.pallas_call(
        rank_kernel,
        in_specs=[WHOLE] * 4,
        out_specs=WHOLE,
        out_shape=jax.ShapeDtypeStruct((CHIPS, BLOCK, COMP + RANK), jnp.bfloat16),
        compiler_params=pltpu.CompilerParams(vmem_limit_bytes=16 * 1024 * 1024),
        cost_estimate=pl.CostEstimate(
            flops=RANK_FLOPS, bytes_accessed=3_600_000, transcendentals=0
        ),
        name="rank_grad_rows",
    )(out_grad, inputs, comp_mat, up_mat)


def on_device(
    top_grad, pooled_in, w_down, w_up, cross_bias, w_comp, feature_slot, bag_ids, bag_lengths
):
    arrived = lax.all_to_all(top_grad, "hst", split_axis=1, concat_axis=0, tiled=True)
    out_grad = arrived.reshape(BLOCK, COMP)
    inputs, down_mat, up_mat, comp_mat = pooled_in[0], w_down[0], w_up[0], w_comp[0]

    partner = lax.ppermute(inputs, "tower", SWAP)
    mine, *sent = call(
        pack_kernel,
        [inputs, partner, down_mat],
        [half_type(*TILE)] + [half_type(2, *TILE)] * NEAR + [half_type(*TILE)],
        "low_rank_and_columns",
        PACK_FLOPS,
        3_000_000,
    )
    received = [
        lax.ppermute(block, "tower", both_ways(step)) for step, block in enumerate(sent, 1)
    ]

    rows_out = rank_rows(out_grad, inputs, comp_mat, up_mat)
    rows_out, ids, lengths = lax.optimization_barrier((rows_out, bag_ids[0, 0], bag_lengths[0]))
    counts, spread = call(
        counts_kernel,
        [jnp.transpose(ids), lengths],
        [half_type(CORES, TABLE_ROWS, HALF), full_type(CORES, HALF, EMBED)],
        "bag_counts",
        COUNTS_FLOPS,
    )
    counts, *received = lax.optimization_barrier((counts, *received))
    grads_own = lax.all_to_all(
        rows_out,
        "tower",
        split_axis=0,
        concat_axis=0,
        tiled=True,
        axis_index_groups=SAME_CORE,
    ).reshape(HALF, COMP + RANK)

    eight = half_type(CHIPS, 3, BLOCK, EMBED)
    (give,) = call(merge_kernel, [mine, *received], [eight], "merge_rows", MERGE_FLOPS)
    taken = lax.ppermute(give, "tower", SWAP)
    low, x, crossed, scale, comp_two, down_one = call(
        saved_kernel,
        [mine, *received, taken, down_mat, up_mat, cross_bias, comp_mat],
        [
            half_type(CORES, HALF, RANK),
            half_type(CORES, HALF, EMBED),
            half_type(CORES, HALF, EMBED),
            full_type(CORES, HALF, EMBED),
            half_type(2 * EMBED, COMP),
            half_type(EMBED, RANK),
        ],
        "saved_rows",
        scalars=[feature_slot],
    )
    saved = (low, x, crossed, scale, counts, spread, comp_two, down_one)
    grads_own, *saved = lax.optimization_barrier((grads_own, *saved))
    grads_other = lax.ppermute(grads_own, "tower", SWAP)
    first = half(0, grads_own, saved)
    grad_down, grad_up, grad_bias, grad_comp, tables = half(1, grads_other, saved, first)
    return grad_down[None], grad_up[None], grad_bias, grad_comp[None], tables[None, None]


def solution(mesh):
    placed = (
        P(("tower", "hst"), None, None),
        P("hst", "tower", None),
        P("hst", None, None),
        P("hst", None, None),
        P("hst", None),
        P("hst", None, None),
        P("hst", None),
        P("hst", "tower", None, None),
        P("hst", "tower", None),
    )
    return jax.shard_map(
        on_device,
        mesh=mesh,
        in_specs=placed,
        out_specs=(
            P("hst", "tower", None),
            P("hst", None, "tower"),
            P("hst", "tower"),
            P("hst", "tower", None),
            P("hst", "tower", None, None),
        ),
        check_vma=False,
    )
```

```python
import jax
import jax.numpy as jnp
from jax import lax
from jax.experimental import pallas as pl
from jax.experimental.pallas import tpu as pltpu
from jax.sharding import PartitionSpec as P

EMBED = 128
COMP = 256
RANK = 256
TABLE_ROWS = 512
SLOTS = 8
CHIPS = 8
CORES = 2
BLOCK = 128
HALF = CHIPS * BLOCK

STEPS = 2
ROOM = 60 * 1024 * 1024
HALF_ROOM = 60 * 1024 * 1024
PACK_FLOPS = 270_000_000
RANK_FLOPS = 270_000_000
MERGE_FLOPS = 16_000_000_000
COUNTS_FLOPS = 2_000_000_000

NEAR = CHIPS // 2 - 1
SAME_CORE = [[chip * CORES + core for chip in range(CHIPS)] for core in range(CORES)]
SWAP = [(t, t ^ 1) for t in range(CHIPS * CORES)]


def both_ways(step):
    pairs = []
    for chip in range(CHIPS):
        pairs.append((chip * CORES, (chip + step) % CHIPS * CORES))
        pairs.append((chip * CORES + 1, (chip - step) % CHIPS * CORES + 1))
    return pairs


def contract_rows(left, right):
    return lax.dot_general(
        left, right, (((0,), (0,)), ((), ())), preferred_element_type=jnp.float32
    )


def contract_cols(left, right):
    return lax.dot_general(
        left, right, (((1,), (1,)), ((), ())), preferred_element_type=jnp.float32
    )


def product(left, right):
    return jnp.dot(left, right, preferred_element_type=jnp.float32)


def half_kernel(*refs):
    grads_ref, low_ref, x_ref, crossed_ref, scale_ref, counts_ref, spread_ref, comp_ref, down_ref = (
        refs[:9]
    )
    before, out_refs, up_sum = refs[9:-6], refs[-6:-1], refs[-1]
    sums = list(out_refs)
    sums[1] = up_sum

    @pl.when(pl.program_id(0) == 0)
    def _():
        for index, ref in enumerate(sums):
            ref[...] = before[index][...] if before else jnp.zeros(ref.shape, ref.dtype)

    out_grad = grads_ref[:, :COMP]
    rank_grad = grads_ref[:, COMP:]
    x = x_ref[0]
    cross = contract_cols(out_grad, comp_ref[...])
    back = contract_cols(rank_grad, down_ref[...])
    input_grad = (cross[:, EMBED:] * scale_ref[0] + back).astype(jnp.bfloat16)
    scaled = input_grad.astype(jnp.float32) * spread_ref[0]
    high = scaled.astype(jnp.bfloat16)
    rest = (scaled - high.astype(jnp.float32)).astype(jnp.bfloat16)
    table = product(counts_ref[0], jnp.concatenate([high, rest], axis=1))
    scale_grad = (cross[:, :EMBED] * x.astype(jnp.float32)).astype(jnp.bfloat16)
    down_out, up_out, bias_out, comp_out, table_out = out_refs
    up_sum[...] += contract_rows(scale_grad, low_ref[0])
    down_out[...] += contract_rows(x, rank_grad)
    bias_out[...] += jnp.sum(scale_grad.astype(jnp.float32), axis=0, keepdims=True)
    comp_out[...] += contract_rows(crossed_ref[0], out_grad)
    table_out[...] += table[:, :EMBED] + table[:, EMBED:]

    @pl.when(pl.program_id(0) == pl.num_programs(0) - 1)
    def _():
        up_out[...] = up_sum[...].T if before else up_sum[...]


def half(side, grads, saved, before=()):
    step = HALF // STEPS
    shapes = [(EMBED, RANK), (EMBED, RANK), (1, EMBED), (EMBED, COMP), (TABLE_ROWS, EMBED)]
    if before:
        shapes[1] = (RANK, EMBED)

    def rows(width):
        return pl.BlockSpec((1, step, width), lambda i: (side, i, 0))

    in_specs = [
        pl.BlockSpec((step, COMP + RANK), lambda i: (i, 0)),
        rows(RANK),
        rows(EMBED),
        rows(EMBED),
        rows(EMBED),
        pl.BlockSpec((1, TABLE_ROWS, step), lambda i: (side, 0, i)),
        rows(EMBED),
        fetched((2 * EMBED, COMP)),
        fetched((EMBED, RANK)),
    ] + [fetched(array.shape) for array in before]
    return pl.pallas_call(
        half_kernel,
        grid=(STEPS,),
        in_specs=in_specs,
        out_specs=[fetched(shape) for shape in shapes],
        out_shape=[full_type(*shape) for shape in shapes],
        scratch_shapes=[pltpu.VMEM((EMBED, RANK), jnp.float32)],
        compiler_params=pltpu.CompilerParams(vmem_limit_bytes=HALF_ROOM),
        cost_estimate=pl.CostEstimate(
            flops=1_500_000_000, bytes_accessed=6_000_000, transcendentals=0
        ),
        name="column_half_second" if before else "column_half_first",
    )(grads, *saved, *before)


def pack_kernel(
    x_ref, partner_ref, down_ref, self_ref, first_ref, second_ref, third_ref, far_ref
):
    _, core, chip = where_am_i()
    way = 1 - 2 * core
    sides = []
    for ref in (x_ref, partner_ref):
        low = product(ref[...], down_ref[...]).astype(jnp.bfloat16)
        sides.append((ref, low))

    def fill(step, side, target):
        ref, low = sides[side]
        base = lax.rem(chip + way * step + CHIPS, CHIPS) * CORES
        for part, slot in ((0, base + core), (3, base + 1 - core)):
            target[part] = ref[:, pl.ds(pl.multiple_of(slot * EMBED, EMBED), EMBED)]
        target[1] = low[:, :BLOCK]
        target[2] = low[:, BLOCK:]

    for step, near_ref in enumerate((first_ref, second_ref, third_ref), 1):
        for side in range(2):
            fill(step, side, near_ref.at[side])
    fill(CHIPS // 2, 0, far_ref)
    fill(0, 0, self_ref)


WHOLE = pl.BlockSpec(memory_space=pltpu.VMEM)
SCALARS = pl.BlockSpec(memory_space=pltpu.SMEM)


def fetched(shape):
    return pl.BlockSpec(shape, lambda i: (0,) * len(shape))


def where_am_i():
    me = lax.axis_index("tower")
    return me, me & 1, me >> 1


def call(kernel, operands, shapes, name, flops=1000, moved=1000, scalars=()):
    return pl.pallas_call(
        kernel,
        grid=(1,),
        in_specs=[SCALARS] * len(scalars) + [fetched(operand.shape) for operand in operands],
        out_specs=[fetched(shape.shape) for shape in shapes],
        out_shape=shapes,
        compiler_params=pltpu.CompilerParams(vmem_limit_bytes=ROOM),
        cost_estimate=pl.CostEstimate(flops=flops, bytes_accessed=moved, transcendentals=0),
        name=name,
    )(*scalars, *operands)


def half_type(*shape):
    return jax.ShapeDtypeStruct(shape, jnp.bfloat16)


def full_type(*shape):
    return jax.ShapeDtypeStruct(shape, jnp.float32)


TILE = (4, BLOCK, EMBED)


def in_order(self_ref, first_ref, second_ref, third_ref, far_ref):
    blocks = [self_ref]
    for ref in (first_ref, second_ref, third_ref):
        blocks += [ref.at[0], ref.at[1]]
    return blocks + [far_ref]


def merge_kernel(*refs):
    give_ref = refs[-1]
    for index, block in enumerate(in_order(*refs[:-1])):
        give_ref[index] = block[1:4]


def counts_kernel(ids_ref, lengths_ref, counts_ref, spread_ref):
    _, mine, _ = where_am_i()
    tile = 64
    middle = TABLE_ROWS // 2
    narrow = jnp.bfloat16

    @pl.loop(0, CHIPS * CORES)
    def _(block):
        side = jnp.where(lax.rem(block, CORES) == mine, 0, 1)
        bags = pl.ds(pl.multiple_of(block * BLOCK, BLOCK), BLOCK)
        to = pl.ds(pl.multiple_of(lax.div(block, CORES) * BLOCK, BLOCK), BLOCK)
        lengths = lengths_ref[:, bags]
        live = [
            jnp.broadcast_to(
                jnp.where(lengths > slot, ids_ref[slot : slot + 1, bags] - middle, TABLE_ROWS)
                .astype(jnp.float32)
                .astype(narrow),
                (tile, BLOCK),
            )
            for slot in range(SLOTS)
        ]
        offsets = lax.broadcasted_iota(jnp.int32, (tile, BLOCK), 0).astype(jnp.float32)
        for start in range(0, TABLE_ROWS, tile):
            row_values = (offsets + float(start - middle)).astype(narrow)
            total = jnp.zeros((tile, BLOCK), narrow)
            for slot in range(SLOTS):
                total = total + jnp.where(live[slot] == row_values, narrow(1), narrow(0))
            counts_ref[side, start : start + tile, to] = total
        spread_ref[side, to, :] = jnp.broadcast_to(
            1.0 / lengths.astype(jnp.float32), (BLOCK, BLOCK)
        ).T


def saved_kernel(
    slots_ref,
    self_ref,
    first_ref,
    second_ref,
    third_ref,
    far_ref,
    taken_ref,
    down_ref,
    up_ref,
    bias_ref,
    comp_ref,
    low_ref,
    x_ref,
    crossed_ref,
    scale_ref,
    comp_out,
    down_out,
):
    me, mine, chip = where_am_i()
    slot = jnp.int32(0)
    for index in range(CHIPS * CORES):
        slot = jnp.where(slots_ref[0, index] == me, index, slot)
    own = pl.ds(pl.multiple_of(me * EMBED, EMBED), EMBED)
    served = pl.ds(pl.multiple_of(slot * EMBED, EMBED), EMBED)
    comp_out[:EMBED, :] = comp_ref[own, :]
    comp_out[EMBED:, :] = comp_ref[served, :]
    down_out[...] = down_ref[served, :]
    ups = jnp.concatenate([up_ref[:, own], up_ref[:, served]], axis=1)
    bias = jnp.concatenate([bias_ref[:, own], bias_ref[:, served]], axis=1)
    kept = in_order(self_ref, first_ref, second_ref, third_ref, far_ref)
    for given in range(2):
        holder = 1 - mine if given else mine
        for index in range(CHIPS):
            near = (index + 1) // 2
            opposite = index % 2 == 0 and index > 0
            side = given ^ opposite
            k = lax.rem(chip + (2 * holder - 1) * near + CHIPS, CHIPS)
            rows = pl.ds(pl.multiple_of(k * BLOCK, BLOCK), BLOCK)
            if given:
                low_low, low_high, x = (taken_ref[index, part] for part in range(3))
            else:
                x, low_low, low_high = (kept[index][part] for part in range(3))
            x_ref[side, rows, :] = x
            low_ref[side, rows, :BLOCK] = low_low
            low_ref[side, rows, BLOCK:] = low_high
    for side in range(CORES):
        scale = product(low_ref[side], ups) + bias
        wide = x_ref[side].astype(jnp.float32)
        crossed_ref[side] = (wide * scale[:, :EMBED] + wide).astype(jnp.bfloat16)
        scale_ref[side] = scale[:, EMBED:] + 1.0


def rank_kernel(grad_ref, x_ref, comp_ref, up_ref, out_ref):
    out_grad = grad_ref[...]
    total = jnp.zeros((BLOCK, RANK), jnp.float32)
    width = 512
    for start in range(0, x_ref.shape[1], width):
        columns = pl.ds(start, width)
        cross = contract_cols(out_grad, comp_ref[columns, :])
        scale_grad = (cross * x_ref[:, columns].astype(jnp.float32)).astype(jnp.bfloat16)
        total += contract_cols(scale_grad, up_ref[:, columns])
    rank_grad = total.astype(jnp.bfloat16)
    for chip in range(CHIPS):
        out_ref[chip, :, :COMP] = out_grad
        out_ref[chip, :, COMP:] = rank_grad


def rank_rows(out_grad, inputs, comp_mat, up_mat):
    return pl.pallas_call(
        rank_kernel,
        in_specs=[WHOLE] * 4,
        out_specs=WHOLE,
        out_shape=jax.ShapeDtypeStruct((CHIPS, BLOCK, COMP + RANK), jnp.bfloat16),
        compiler_params=pltpu.CompilerParams(vmem_limit_bytes=16 * 1024 * 1024),
        cost_estimate=pl.CostEstimate(
            flops=RANK_FLOPS, bytes_accessed=3_600_000, transcendentals=0
        ),
        name="rank_grad_rows",
    )(out_grad, inputs, comp_mat, up_mat)


def on_device(
    top_grad, pooled_in, w_down, w_up, cross_bias, w_comp, feature_slot, bag_ids, bag_lengths
):
    arrived = lax.all_to_all(top_grad, "hst", split_axis=1, concat_axis=0, tiled=True)
    out_grad = arrived.reshape(BLOCK, COMP)
    inputs, down_mat, up_mat, comp_mat = pooled_in[0], w_down[0], w_up[0], w_comp[0]

    partner = lax.ppermute(inputs, "tower", SWAP)
    mine, *sent = call(
        pack_kernel,
        [inputs, partner, down_mat],
        [half_type(*TILE)] + [half_type(2, *TILE)] * NEAR + [half_type(*TILE)],
        "low_rank_and_columns",
        PACK_FLOPS,
        3_000_000,
    )
    received = [
        lax.ppermute(block, "tower", both_ways(step)) for step, block in enumerate(sent, 1)
    ]

    rows_out = rank_rows(out_grad, inputs, comp_mat, up_mat)
    rows_out, ids, lengths = lax.optimization_barrier((rows_out, bag_ids[0, 0], bag_lengths[0]))
    counts, spread = call(
        counts_kernel,
        [jnp.transpose(ids), lengths],
        [half_type(CORES, TABLE_ROWS, HALF), full_type(CORES, HALF, EMBED)],
        "bag_counts",
        COUNTS_FLOPS,
    )
    counts, *received = lax.optimization_barrier((counts, *received))
    grads_own = lax.all_to_all(
        rows_out,
        "tower",
        split_axis=0,
        concat_axis=0,
        tiled=True,
        axis_index_groups=SAME_CORE,
    ).reshape(HALF, COMP + RANK)

    eight = half_type(CHIPS, 3, BLOCK, EMBED)
    (give,) = call(merge_kernel, [mine, *received], [eight], "merge_rows", MERGE_FLOPS)
    taken = lax.ppermute(give, "tower", SWAP)
    low, x, crossed, scale, comp_two, down_one = call(
        saved_kernel,
        [mine, *received, taken, down_mat, up_mat, cross_bias, comp_mat],
        [
            half_type(CORES, HALF, RANK),
            half_type(CORES, HALF, EMBED),
            half_type(CORES, HALF, EMBED),
            full_type(CORES, HALF, EMBED),
            half_type(2 * EMBED, COMP),
            half_type(EMBED, RANK),
        ],
        "saved_rows",
        scalars=[feature_slot],
    )
    saved = (low, x, crossed, scale, counts, spread, comp_two, down_one)
    grads_own, *saved = lax.optimization_barrier((grads_own, *saved))
    grads_other = lax.ppermute(grads_own, "tower", SWAP)
    first = half(0, grads_own, saved)
    grad_down, grad_up, grad_bias, grad_comp, tables = half(1, grads_other, saved, first)
    return grad_down[None], grad_up[None], grad_bias, grad_comp[None], tables[None, None]


def solution(mesh):
    placed = (
        P(("tower", "hst"), None, None),
        P("hst", "tower", None),
        P("hst", None, None),
        P("hst", None, None),
        P("hst", None),
        P("hst", None, None),
        P("hst", None),
        P("hst", "tower", None, None),
        P("hst", "tower", None),
    )
    return jax.shard_map(
        on_device,
        mesh=mesh,
        in_specs=placed,
        out_specs=(
            P("hst", "tower", None),
            P("hst", None, "tower"),
            P("hst", "tower"),
            P("hst", "tower", None),
            P("hst", "tower", None, None),
        ),
        check_vma=False,
    )
```

```python
import jax
import jax.numpy as jnp
from jax import lax
from jax.experimental import pallas as pl
from jax.experimental.pallas import tpu as pltpu
from jax.sharding import PartitionSpec as P

EMBED = 128
COMP = 256
RANK = 256
TABLE_ROWS = 512
SLOTS = 8
CHIPS = 8
CORES = 2
BLOCK = 128
HALF = CHIPS * BLOCK

STEPS = 1
ROOM = 60 * 1024 * 1024
PACK_FLOPS = 270_000_000
RANK_FLOPS = 270_000_000
MERGE_FLOPS = 16_000_000_000
COUNTS_FLOPS = 500_000_000

NEAR = CHIPS // 2 - 1
SAME_CORE = [[chip * CORES + core for chip in range(CHIPS)] for core in range(CORES)]
SWAP = [(t, t ^ 1) for t in range(CHIPS * CORES)]


def both_ways(step):
    pairs = []
    for chip in range(CHIPS):
        pairs.append((chip * CORES, (chip + step) % CHIPS * CORES))
        pairs.append((chip * CORES + 1, (chip - step) % CHIPS * CORES + 1))
    return pairs


def contract_rows(left, right):
    return lax.dot_general(
        left, right, (((0,), (0,)), ((), ())), preferred_element_type=jnp.float32
    )


def contract_cols(left, right):
    return lax.dot_general(
        left, right, (((1,), (1,)), ((), ())), preferred_element_type=jnp.float32
    )


def product(left, right):
    return jnp.dot(left, right, preferred_element_type=jnp.float32)


def columns_kernel(
    own_ref,
    other_ref,
    low_ref,
    x_ref,
    crossed_ref,
    scale_ref,
    counts_ref,
    spread_ref,
    comp_ref,
    down_ref,
    down_out,
    up_out,
    bias_out,
    comp_out,
    table_out,
    up_sum,
):
    step = pl.program_id(0)

    @pl.when(step == 0)
    def _():
        for ref in (down_out, up_sum, bias_out, comp_out, table_out):
            ref[...] = jnp.zeros(ref.shape, ref.dtype)

    def add(grads_ref):
        out_grad = grads_ref[:, :COMP]
        rank_grad = grads_ref[:, COMP:]
        x = x_ref[0]
        cross = contract_cols(out_grad, comp_ref[...])
        back = contract_cols(rank_grad, down_ref[...])
        input_grad = (cross[:, EMBED:] * scale_ref[0] + back).astype(jnp.bfloat16)
        scaled = input_grad.astype(jnp.float32) * spread_ref[0]
        high = scaled.astype(jnp.bfloat16)
        rest = (scaled - high.astype(jnp.float32)).astype(jnp.bfloat16)
        table = product(counts_ref[0], jnp.concatenate([high, rest], axis=1))
        scale_grad = (cross[:, :EMBED] * x.astype(jnp.float32)).astype(jnp.bfloat16)
        down_out[...] += contract_rows(x, rank_grad)
        up_sum[...] += contract_rows(scale_grad, low_ref[0])
        bias_out[...] += jnp.sum(scale_grad.astype(jnp.float32), axis=0, keepdims=True)
        comp_out[...] += contract_rows(crossed_ref[0], out_grad)
        table_out[...] += table[:, :EMBED] + table[:, EMBED:]

    @pl.when(step < STEPS)
    def _():
        add(own_ref)

    @pl.when(step >= STEPS)
    def _():
        add(other_ref)

    @pl.when(step == CORES * STEPS - 1)
    def _():
        up_out[...] = up_sum[...].T


def columns(own, other, saved):
    step = HALF // STEPS
    shapes = [(EMBED, RANK), (RANK, EMBED), (1, EMBED), (EMBED, COMP), (TABLE_ROWS, EMBED)]

    def rows(width):
        return pl.BlockSpec((1, step, width), lambda i: (i // STEPS, i % STEPS, 0))

    return pl.pallas_call(
        columns_kernel,
        grid=(CORES * STEPS,),
        in_specs=[
            pl.BlockSpec((step, COMP + RANK), lambda i: (jnp.minimum(i, STEPS - 1), 0)),
            pl.BlockSpec((step, COMP + RANK), lambda i: (jnp.maximum(i - STEPS, 0), 0)),
            rows(RANK),
            rows(EMBED),
            rows(EMBED),
            rows(EMBED),
            pl.BlockSpec((1, TABLE_ROWS, step), lambda i: (i // STEPS, 0, i % STEPS)),
            rows(EMBED),
            fetched((2 * EMBED, COMP)),
            fetched((EMBED, RANK)),
        ],
        out_specs=[fetched(shape) for shape in shapes],
        out_shape=[full_type(*shape) for shape in shapes],
        scratch_shapes=[pltpu.VMEM((EMBED, RANK), jnp.float32)],
        compiler_params=pltpu.CompilerParams(vmem_limit_bytes=ROOM),
        cost_estimate=pl.CostEstimate(
            flops=3_000_000_000, bytes_accessed=12_000_000, transcendentals=0
        ),
        name="column_sums",
    )(own, other, *saved)


def pack_kernel(
    x_ref, partner_ref, down_ref, self_ref, first_ref, second_ref, third_ref, far_ref
):
    _, core, chip = where_am_i()
    way = 1 - 2 * core
    sides = []
    for ref in (x_ref, partner_ref):
        low = product(ref[...], down_ref[...]).astype(jnp.bfloat16)
        sides.append((ref, low))

    def fill(step, side, target):
        ref, low = sides[side]
        base = lax.rem(chip + way * step + CHIPS, CHIPS) * CORES
        for part, slot in ((0, base + core), (3, base + 1 - core)):
            target[part] = ref[:, pl.ds(pl.multiple_of(slot * EMBED, EMBED), EMBED)]
        target[1] = low[:, :BLOCK]
        target[2] = low[:, BLOCK:]

    for step, near_ref in enumerate((first_ref, second_ref, third_ref), 1):
        for side in range(2):
            fill(step, side, near_ref.at[side])
    fill(CHIPS // 2, 0, far_ref)
    fill(0, 0, self_ref)


WHOLE = pl.BlockSpec(memory_space=pltpu.VMEM)
SCALARS = pl.BlockSpec(memory_space=pltpu.SMEM)


def fetched(shape):
    return pl.BlockSpec(shape, lambda i: (0,) * len(shape))


def where_am_i():
    me = lax.axis_index("tower")
    return me, me & 1, me >> 1


def call(kernel, operands, shapes, name, flops=1000, moved=1000, scalars=()):
    return pl.pallas_call(
        kernel,
        grid=(1,),
        in_specs=[SCALARS] * len(scalars) + [fetched(operand.shape) for operand in operands],
        out_specs=[fetched(shape.shape) for shape in shapes],
        out_shape=shapes,
        compiler_params=pltpu.CompilerParams(vmem_limit_bytes=ROOM),
        cost_estimate=pl.CostEstimate(flops=flops, bytes_accessed=moved, transcendentals=0),
        name=name,
    )(*scalars, *operands)


def half_type(*shape):
    return jax.ShapeDtypeStruct(shape, jnp.bfloat16)


def full_type(*shape):
    return jax.ShapeDtypeStruct(shape, jnp.float32)


TILE = (4, BLOCK, EMBED)


def in_order(self_ref, first_ref, second_ref, third_ref, far_ref):
    blocks = [self_ref]
    for ref in (first_ref, second_ref, third_ref):
        blocks += [ref.at[0], ref.at[1]]
    return blocks + [far_ref]


def merge_kernel(*refs):
    give_ref = refs[-1]
    for index, block in enumerate(in_order(*refs[:-1])):
        give_ref[index] = block[1:4]


def counts_kernel(ids_ref, lengths_ref, counts_ref, spread_ref):
    _, mine, _ = where_am_i()
    tile = 64
    middle = TABLE_ROWS // 2
    narrow = jnp.bfloat16

    @pl.loop(0, CHIPS * CORES)
    def _(block):
        side = jnp.where(lax.rem(block, CORES) == mine, 0, 1)
        bags = pl.ds(pl.multiple_of(block * BLOCK, BLOCK), BLOCK)
        to = pl.ds(pl.multiple_of(lax.div(block, CORES) * BLOCK, BLOCK), BLOCK)
        lengths = lengths_ref[:, bags]
        live = [
            jnp.broadcast_to(
                jnp.where(lengths > slot, ids_ref[slot : slot + 1, bags] - middle, TABLE_ROWS)
                .astype(jnp.float32)
                .astype(narrow),
                (tile, BLOCK),
            )
            for slot in range(SLOTS)
        ]
        offsets = lax.broadcasted_iota(jnp.int32, (tile, BLOCK), 0).astype(jnp.float32)
        for start in range(0, TABLE_ROWS, tile):
            row_values = (offsets + float(start - middle)).astype(narrow)
            total = jnp.zeros((tile, BLOCK), narrow)
            for slot in range(SLOTS):
                total = total + jnp.where(live[slot] == row_values, narrow(1), narrow(0))
            counts_ref[side, start : start + tile, to] = total
        spread_ref[side, to, :] = jnp.broadcast_to(
            1.0 / lengths.astype(jnp.float32), (BLOCK, BLOCK)
        ).T


def saved_kernel(
    slots_ref,
    self_ref,
    first_ref,
    second_ref,
    third_ref,
    far_ref,
    taken_ref,
    down_ref,
    up_ref,
    bias_ref,
    comp_ref,
    low_ref,
    x_ref,
    crossed_ref,
    scale_ref,
    comp_out,
    down_out,
):
    me, mine, chip = where_am_i()
    slot = jnp.int32(0)
    for index in range(CHIPS * CORES):
        slot = jnp.where(slots_ref[0, index] == me, index, slot)
    own = pl.ds(pl.multiple_of(me * EMBED, EMBED), EMBED)
    served = pl.ds(pl.multiple_of(slot * EMBED, EMBED), EMBED)
    comp_out[:EMBED, :] = comp_ref[own, :]
    comp_out[EMBED:, :] = comp_ref[served, :]
    down_out[...] = down_ref[served, :]
    ups = jnp.concatenate([up_ref[:, own], up_ref[:, served]], axis=1)
    bias = jnp.concatenate([bias_ref[:, own], bias_ref[:, served]], axis=1)
    kept = in_order(self_ref, first_ref, second_ref, third_ref, far_ref)
    for given in range(2):
        holder = 1 - mine if given else mine
        for index in range(CHIPS):
            near = (index + 1) // 2
            opposite = index % 2 == 0 and index > 0
            side = given ^ opposite
            k = lax.rem(chip + (2 * holder - 1) * near + CHIPS, CHIPS)
            rows = pl.ds(pl.multiple_of(k * BLOCK, BLOCK), BLOCK)
            if given:
                low_low, low_high, x = (taken_ref[index, part] for part in range(3))
            else:
                x, low_low, low_high = (kept[index][part] for part in range(3))
            x_ref[side, rows, :] = x
            low_ref[side, rows, :BLOCK] = low_low
            low_ref[side, rows, BLOCK:] = low_high
    for side in range(CORES):
        scale = product(low_ref[side], ups) + bias
        wide = x_ref[side].astype(jnp.float32)
        crossed_ref[side] = (wide * scale[:, :EMBED] + wide).astype(jnp.bfloat16)
        scale_ref[side] = scale[:, EMBED:] + 1.0


def rank_kernel(grad_ref, x_ref, comp_ref, up_ref, out_ref):
    out_grad = grad_ref[...]
    total = jnp.zeros((BLOCK, RANK), jnp.float32)
    width = 512
    for start in range(0, x_ref.shape[1], width):
        columns = pl.ds(start, width)
        cross = contract_cols(out_grad, comp_ref[columns, :])
        scale_grad = (cross * x_ref[:, columns].astype(jnp.float32)).astype(jnp.bfloat16)
        total += contract_cols(scale_grad, up_ref[:, columns])
    rank_grad = total.astype(jnp.bfloat16)
    for chip in range(CHIPS):
        out_ref[chip, :, :COMP] = out_grad
        out_ref[chip, :, COMP:] = rank_grad


def rank_rows(out_grad, inputs, comp_mat, up_mat):
    return pl.pallas_call(
        rank_kernel,
        in_specs=[WHOLE] * 4,
        out_specs=WHOLE,
        out_shape=jax.ShapeDtypeStruct((CHIPS, BLOCK, COMP + RANK), jnp.bfloat16),
        compiler_params=pltpu.CompilerParams(vmem_limit_bytes=16 * 1024 * 1024),
        cost_estimate=pl.CostEstimate(
            flops=RANK_FLOPS, bytes_accessed=3_600_000, transcendentals=0
        ),
        name="rank_grad_rows",
    )(out_grad, inputs, comp_mat, up_mat)


def on_device(
    top_grad, pooled_in, w_down, w_up, cross_bias, w_comp, feature_slot, bag_ids, bag_lengths
):
    arrived = lax.all_to_all(top_grad, "hst", split_axis=1, concat_axis=0, tiled=True)
    out_grad = arrived.reshape(BLOCK, COMP)
    inputs, down_mat, up_mat, comp_mat = pooled_in[0], w_down[0], w_up[0], w_comp[0]

    partner = lax.ppermute(inputs, "tower", SWAP)
    mine, *sent = call(
        pack_kernel,
        [inputs, partner, down_mat],
        [half_type(*TILE)] + [half_type(2, *TILE)] * NEAR + [half_type(*TILE)],
        "low_rank_and_columns",
        PACK_FLOPS,
        3_000_000,
    )
    received = [
        lax.ppermute(block, "tower", both_ways(step)) for step, block in enumerate(sent, 1)
    ]

    rows_out = rank_rows(out_grad, inputs, comp_mat, up_mat)
    rows_out, ids, lengths = lax.optimization_barrier((rows_out, bag_ids[0, 0], bag_lengths[0]))
    counts, spread = call(
        counts_kernel,
        [jnp.transpose(ids), lengths],
        [half_type(CORES, TABLE_ROWS, HALF), full_type(CORES, HALF, EMBED)],
        "bag_counts",
        COUNTS_FLOPS,
    )
    counts, *received = lax.optimization_barrier((counts, *received))
    grads_own = lax.all_to_all(
        rows_out,
        "tower",
        split_axis=0,
        concat_axis=0,
        tiled=True,
        axis_index_groups=SAME_CORE,
    ).reshape(HALF, COMP + RANK)

    eight = half_type(CHIPS, 3, BLOCK, EMBED)
    (give,) = call(merge_kernel, [mine, *received], [eight], "merge_rows", MERGE_FLOPS)
    taken = lax.ppermute(give, "tower", SWAP)
    low, x, crossed, scale, comp_two, down_one = call(
        saved_kernel,
        [mine, *received, taken, down_mat, up_mat, cross_bias, comp_mat],
        [
            half_type(CORES, HALF, RANK),
            half_type(CORES, HALF, EMBED),
            half_type(CORES, HALF, EMBED),
            full_type(CORES, HALF, EMBED),
            half_type(2 * EMBED, COMP),
            half_type(EMBED, RANK),
        ],
        "saved_rows",
        scalars=[feature_slot],
    )
    saved = (low, x, crossed, scale, counts, spread, comp_two, down_one)
    grads_own, *saved = lax.optimization_barrier((grads_own, *saved))
    grads_other = lax.ppermute(grads_own, "tower", SWAP)
    grad_down, grad_up, grad_bias, grad_comp, tables = columns(grads_own, grads_other, saved)
    return grad_down[None], grad_up[None], grad_bias, grad_comp[None], tables[None, None]


def solution(mesh):
    placed = (
        P(("tower", "hst"), None, None),
        P("hst", "tower", None),
        P("hst", None, None),
        P("hst", None, None),
        P("hst", None),
        P("hst", None, None),
        P("hst", None),
        P("hst", "tower", None, None),
        P("hst", "tower", None),
    )
    return jax.shard_map(
        on_device,
        mesh=mesh,
        in_specs=placed,
        out_specs=(
            P("hst", "tower", None),
            P("hst", None, "tower"),
            P("hst", "tower"),
            P("hst", "tower", None),
            P("hst", "tower", None, None),
        ),
        check_vma=False,
    )
```
